1024 devices in a mesh: band: 256 (over x, y, z_lo, core), lev: 4 (over z_hi).
Axes of the slice: x: 4, y: 8, z: 16 (z_hi: 4, z_lo: 4; z = z_hi * 4 + z_lo), core: 2. Of those that a mesh axis runs over, the one named last changes fastest.
Arguments:
- spectral: bfloat16 [1280, 2, 4, 3, 1280], P('band', None, 'lev'), may hold values from -0.08984375 to 0.08984375
- legendre: bfloat16 [1280, 256, 1280], P('band'), may hold values from -0.15625 to 0.15625
- level_weights: float32 [4], P('lev'), may hold values from 0.1 to 0.6
- coupling: int32 [1024, 128], P('band'), may hold values from 0 to 131071
- land_sea: int32 [1024, 128], P('band'), may hold values 0 or 1
- spectra: bfloat16 [36, 36, 1024, 128], P('lev', None, 'band'), may hold values from 0.049804688 to 2
- courant: float32 [36], P('lev'), may hold values from 0.1 to 0.65
- growth_rate: float32 [36], P('lev'), may hold values from 0.05 to 0.5
- breaking: float32 [36], P('lev'), may hold values from 0.1 to 1
Outputs:
- grid: float32 [256, 4, 3, 512], P('band', 'lev')
- spectra_out: float32 [36, 36, 1024, 128], P('lev', None, 'band')
- charnock: float32 [1024, 128], P('band')
The draws below stay inside these ranges and needn't reach their ends.
All inputs are finite; a program needn't handle non-finite values. No bound on the sum of `land_sea` on one device may be relied on, other than what follows from the above.
Results may differ from the reference program's by a relative error of at most 0.0029.
Values may be sent and summed in bfloat16 or wider, within the bound.
A program may use at most 32 MiB of HBM per device.

```python
import math
import jax
import jax.numpy as jnp
from jax import lax

M = 1280
N = 1280
NLON = 5136
LON_W = 512
NF = 36
ND = 36
WC = 128
STEPS = 4
NLAT_W = 256
LEVELS = 4
WROWS = 1024
N_BAND = 256


def touch_ends(values, stream_key, low, largest):
    longest = values.shape.index(max(values.shape))
    spots = []
    for shift in (0, 1):
        where = [jax.random.randint(jax.random.fold_in(stream_key, axis), (), 0, length) for axis, length in enumerate(values.shape)]
        where[longest] = (where[longest] + shift) % values.shape[longest]
        spots.append(tuple(where))
    return values.at[spots[0]].set(low).at[spots[1]].set(largest)


def block_levels(rng, dims, pieces, smallest, largest):
    def one(axis_at, parts):
        heights = jax.random.uniform(jax.random.fold_in(jax.random.fold_in(rng, 6), axis_at), (parts,), jnp.float32, smallest / len(pieces), largest / len(pieces))
        return jnp.repeat(jnp.exp(heights), dims[axis_at] // parts).reshape((-1,) + (1,) * (len(dims) - axis_at - 1))

    gain = one(*pieces[0])
    for cut in pieces[1:]:
        gain = gain * one(*cut)
    return gain


def bell_draw(own_key, shape, width, most, cuts=(), held_as=jnp.bfloat16):
    loudness = block_levels(own_key, shape, cuts, -0.22, 0.18) if cuts else 1.0
    entries = jax.random.normal(own_key, shape, jnp.float32) * width * loudness
    return jnp.minimum(jnp.maximum(entries, -most), most).astype(held_as)


def setup_inputs(seed: int = 0) -> dict:
    arg_keys = jax.random.split(jax.random.key(seed), 10)
    spectral = bell_draw(arg_keys[0], (M, 2, LEVELS, 3, N), 0.014, 0.08984375, ((0, 256), (2, 4)))
    legendre = bell_draw(arg_keys[1], (M, NLAT_W, N), N ** -0.5, 0.15625, ((0, 256),))
    level_weights = jnp.clip(jnp.exp(math.log(0.6) - 1.7917595 * jax.random.uniform(arg_keys[2], (LEVELS,), jnp.float32) ** block_levels(arg_keys[2], (LEVELS,), ((0, 4),), -0.2, 0.2)), 0.1, 0.6)
    coupling = touch_ends(jax.random.randint(arg_keys[3], (WROWS, WC), 0, NLAT_W * LON_W), jax.random.fold_in(arg_keys[3], 1), 0, (NLAT_W * LON_W) - 1).astype(jnp.int32)
    land_sea = touch_ends((jax.random.randint(arg_keys[4], (WROWS, WC), 0, 4) < 3).astype(jnp.int32), jax.random.fold_in(arg_keys[4], 1), 0, 1)
    spectra = jnp.clip(jnp.exp(math.log(2.0) - 3.6927934 * jax.random.uniform(arg_keys[5], (NF, ND, WROWS, WC), jnp.float32) ** block_levels(arg_keys[5], (NF, ND, WROWS, WC), ((0, 4), (2, 256)), -0.2, 0.2)), 0.049804688, 2.0).astype(jnp.bfloat16)
    courant = jnp.clip(jnp.exp(math.log(0.65) - 1.8718021 * jax.random.uniform(arg_keys[6], (NF,), jnp.float32) ** block_levels(arg_keys[6], (NF,), ((0, 4),), -0.2, 0.2)), 0.1, 0.65)
    growth_rate = jnp.clip(jnp.exp(math.log(0.5) - 2.3025851 * jax.random.uniform(arg_keys[7], (NF,), jnp.float32) ** block_levels(arg_keys[7], (NF,), ((0, 4),), -0.2, 0.2)), 0.05, 0.5)
    breaking = jnp.clip(jnp.exp(math.log(1.0) - 2.3025851 * jax.random.uniform(arg_keys[8], (NF,), jnp.float32) ** block_levels(arg_keys[8], (NF,), ((0, 4),), -0.2, 0.2)), 0.1, 1.0)
    return dict(spectral=spectral, legendre=legendre, level_weights=level_weights, coupling=coupling, land_sea=land_sea, spectra=spectra, courant=courant, growth_rate=growth_rate, breaking=breaking)


def fourier_basis(first, count):
    waves = first + jnp.arange(count, dtype=jnp.int32)
    columns = jnp.arange(LON_W, dtype=jnp.int32)
    remains = (waves[:, None] * columns[None, :]) % NLON
    angles = (2.0 * math.pi / NLON) * remains.astype(jnp.float32)
    weights = jnp.where(waves == 0, 1.0, 2.0).astype(jnp.float32)[:, None]
    return jnp.stack([weights * jnp.cos(angles), -weights * jnp.sin(angles)])


def advance(padded, east_speed, north_speed):
    centre = padded[..., 1:-1, :]
    below = padded[..., :-2, :]
    above = padded[..., 2:, :]
    west = jnp.roll(centre, 1, axis=-1)
    east = jnp.roll(centre, -1, axis=-1)
    return (centre - jnp.maximum(east_speed, 0.0) * (centre - west)
            - jnp.minimum(east_speed, 0.0) * (east - centre)
            - jnp.maximum(north_speed, 0.0) * (centre - below)
            - jnp.minimum(north_speed, 0.0) * (above - centre))


def reference(spectral, legendre, level_weights, coupling, land_sea, spectra, courant, growth_rate, breaking):
    blocks = N_BAND
    block_size = M // blocks
    table = legendre.reshape(blocks, block_size, NLAT_W, N)
    stacked = spectral.reshape(blocks, block_size, 2 * LEVELS * 3, N)

    def one_block(pair):
        return lax.dot_general(pair[1], pair[0], (((2,), (2,)), ((0,), (0,))),
                               preferred_element_type=jnp.float32).astype(jnp.bfloat16)

    legendre_out = lax.map(one_block, (table, stacked)).reshape(M, 2, LEVELS * 3, NLAT_W)
    legendre_out = lax.optimization_barrier(legendre_out)
    basis = fourier_basis(0, M)
    grid = jnp.einsum("mrfl,rmx->lfx", legendre_out.astype(jnp.float32), basis,
                      precision=lax.Precision.HIGHEST)
    grid = grid.reshape(NLAT_W, LEVELS, 3, LON_W)
    wind = jnp.sum(grid[:, :, 0:2, :] * level_weights[None, :, None, None], axis=1)
    wind_east = jnp.take(wind[:, 0, :].reshape(-1), coupling)
    wind_north = jnp.take(wind[:, 1, :].reshape(-1), coupling)

    theta = (2.0 * math.pi / ND) * (jnp.arange(ND).astype(jnp.float32) + 0.5)
    cosines = jnp.cos(theta)[:, None, None]
    sines = jnp.sin(theta)[:, None, None]
    push = jnp.maximum(cosines * wind_east[None] + sines * wind_north[None], 0.0)
    landmask = land_sea.astype(jnp.float32)
    energy = 1.0 + 2.0 * jnp.arange(NF).astype(jnp.float32) / (NF - 1)

    def one_frequency(items):
        field, speed, rate, damping, weight = items
        state = field.astype(jnp.float32)
        for step in range(STEPS):
            padded = jnp.pad(state, ((0, 0), (1, 1), (0, 0)))
            state = advance(padded, speed * cosines, speed * sines)
        growth = rate * push
        result = landmask * state * (1.0 + growth) / (1.0 + damping * state)
        partial_value = weight * jnp.sum(growth * state, axis=0) * landmask
        return result, partial_value

    spectra_out, partials = lax.map(one_frequency, (spectra, courant, growth_rate, breaking, energy))
    stress = jnp.sum(partials, axis=0) / (NF * ND)
    charnock = 0.011 + 0.5 * stress / (stress + 0.05 * (1.0 + wind_east * wind_east + wind_north * wind_north))
    return grid, spectra_out, charnock
```

```python
import math

import jax
import jax.numpy as jnp
from jax import lax
from jax.experimental import pallas as pl
from jax.experimental.pallas import tpu as pltpu
from jax.sharding import PartitionSpec as P

N = 1280
NLON = 5136
LON_W = 512
NLAT = 256
NF = 36
ND = 36
STEPS = 4
NX, NY, NZC, NV = 4, 8, 8, 4
NB = NX * NY * NZC
NR = NX * NZC
NC = NY * NV
MESH = pl.DeviceIdType.MESH
F32, BF16 = jnp.float32, jnp.bfloat16


def turn(t):
    u = (t - jnp.floor(t + 0.5)) * (2.0 * math.pi)
    s = u * u
    even = jnp.full_like(u, 1.0 / math.factorial(16))
    odd = jnp.full_like(u, -1.0 / math.factorial(17 - 2))
    for k in range(7, -1, -1):
        even = even * s + (-1.0) ** k / math.factorial(2 * k)
        if k < 7:
            odd = odd * s + (-1.0) ** k / math.factorial(2 * k + 1)
    return even, u * odd


def cycles(product):
    return (product - jnp.floor(product * (1.0 / NLON)) * NLON) * (1.0 / NLON)


def kernel(
    spec, leg, lw, coup, land, spectra, cour_h, rate_h, brk_h,
    grid_o, out_o, char_o,
    leg_v, spec_v, coup_v, land_v, own_v, s32, proj, send1, recv1, pack, send2, recv2,
    rhs, ebuf, wsend, wrecv, onehot, rsend, rrecv, halo, ext, trig, state, tsum, stsend, strecv, res,
    cour, rate, brk,
    leg_s, in_s, out_s, s1, r1, s2, r2, sw, rw, sr, rr, sh, rh, sc, rc, ss, rs,
):
    b = lax.axis_index("band")
    v = lax.axis_index("lev")
    x = b // 64
    y = lax.rem(b // 8, 8)
    zc = lax.rem(b, 8)
    row = x * NZC + zc
    col = y * NV + v
    up = lax.rem(b + 1, NB)
    down = lax.rem(b + NB - 1, NB)

    def in_row(j):
        return (j // NZC) * (NY * NZC) + y * NZC + lax.rem(j, NZC)

    def in_col(j):
        return x * (NY * NZC) + (j // NV) * NZC + zc

    loads = [pltpu.make_async_copy(leg.at[m], leg_v.at[m], leg_s.at[m]) for m in range(5)]
    spec_c = pltpu.make_async_copy(spec, spec_v, in_s.at[0])
    coup_c = pltpu.make_async_copy(coup, coup_v.at[y], in_s.at[1])
    land_c = pltpu.make_async_copy(land, land_v, in_s.at[2])
    own_c = pltpu.make_async_copy(spectra, own_v, in_s.at[3])
    spec_c.start()
    for c in loads:
        c.start()
    coup_c.start()
    land_c.start()
    own_c.start()
    scalars = [
        pltpu.make_async_copy(h, t, in_s.at[4 + i])
        for i, (h, t) in enumerate(((cour_h, cour), (rate_h, rate), (brk_h, brk)))
    ]
    for c in scalars:
        c.start()

    with jax.named_scope("greet"):
        barrier = pltpu.get_barrier_semaphore()

        def greet_row(j, _):
            t = in_row(lax.rem(row + j, NR))
            pl.semaphore_signal(barrier, inc=1, device_id={"band": t, "lev": v}, device_id_type=MESH)
            return 0

        def greet_col(j, _):
            g = lax.rem(col + j, NC)
            pl.semaphore_signal(
                barrier, inc=1, device_id={"band": in_col(g), "lev": lax.rem(g, NV)}, device_id_type=MESH
            )
            return 0

        lax.fori_loop(1, NR, greet_row, 0)
        lax.fori_loop(1, NC, greet_col, 0)
        pl.semaphore_signal(barrier, inc=1, device_id={"band": up, "lev": v}, device_id_type=MESH)
        pl.semaphore_signal(barrier, inc=1, device_id={"band": down, "lev": v}, device_id_type=MESH)

    with jax.named_scope("tables"):
        slot = lax.broadcasted_iota(jnp.int32, (128, LON_W), 0)
        lon = lax.broadcasted_iota(jnp.int32, (128, LON_W), 1).astype(F32)
        xs = slot >> 5
        slot = slot & 31
        mi = (slot * 43) >> 8
        k = (xs * 320 + mi).astype(F32)
        part = (slot & 1).astype(F32)
        re, im = turn(cycles(k * lon) + 0.25 * part)
        re_hi, im_hi = re.astype(BF16), im.astype(BF16)
        rhs[0:128, 0:LON_W] = re_hi
        rhs[0:128, LON_W:] = im_hi
        rhs[128:256, 0:LON_W] = (re - re_hi.astype(F32)).astype(BF16)
        rhs[128:256, LON_W:] = (im - im_hi.astype(F32)).astype(BF16)
        q = lax.broadcasted_iota(jnp.int32, (64, LON_W), 0).astype(F32)
        lon = lax.broadcasted_iota(jnp.int32, (64, LON_W), 1).astype(F32)
        ec, es = turn(cycles(q * 5.0 * lon))
        ebuf[0] = 2.0 * ec
        ebuf[1] = 2.0 * es
        e = lax.broadcasted_iota(jnp.int32, (18, 8, 128), 0).astype(F32)
        tc, ts = turn((e + 0.5) * (1.0 / ND))
        trig[0] = tc
        trig[1] = ts

    with jax.named_scope("rows"):
        spec_c.wait()
        s32[30:32, :] = jnp.zeros((2, N), F32)
        for j in range(15):
            s32[2 * j : 2 * j + 2, :] = spec_v[j].astype(F32)

    with jax.named_scope("entry_wait"):
        pl.semaphore_wait(barrier, NR - 1 + NC - 1 + 2)

    with jax.named_scope("halo_sends"):
        half = ND // 2
        halo_up = pltpu.make_async_remote_copy(
            src_ref=spectra.at[:, 0:half], dst_ref=halo.at[0], send_sem=sh.at[0], recv_sem=rh.at[0],
            device_id={"band": up, "lev": v}, device_id_type=MESH)
        halo_down = pltpu.make_async_remote_copy(
            src_ref=spectra.at[:, half:], dst_ref=halo.at[1], send_sem=sh.at[1], recv_sem=rh.at[1],
            device_id={"band": down, "lev": v}, device_id_type=MESH)
        halo_up.start()
        halo_down.start()

        def send_coup(j, _):
            t = lax.rem(y + j, NY)
            pltpu.make_async_remote_copy(
                src_ref=coup, dst_ref=coup_v.at[y], send_sem=sc, recv_sem=rc,
                device_id={"band": x * (NY * NZC) + t * NZC + zc, "lev": v}, device_id_type=MESH).start()
            return 0

        lax.fori_loop(1, NY, send_coup, 0)

    with jax.named_scope("legendre"):
        sl = lax.broadcasted_iota(jnp.int32, (128, N), 0)
        held = s32[...]
        held = jnp.concatenate([held, held, held, held], axis=0)
        sx = sl >> 5
        sm = ((sl & 31) * 43) >> 8
        held = jnp.where(sx == x, held, 0.0)
        acc = None
        for m in range(5):
            loads[m].wait()
            s_m = jnp.where(sm == m, held, 0.0).astype(BF16)
            d = lax.dot_general(leg_v[m], s_m, (((1,), (1,)), ((), ())), preferred_element_type=F32)
            acc = d if acc is None else acc + d
        proj[...] = acc.astype(BF16).astype(F32)
        for j in range(NR):
            send1[j] = proj[pl.ds((j // NZC) * 64 + j % NZC, NY, stride=NZC), :]

    with jax.named_scope("first_sends"):
        def send_1(j, _):
            t = lax.rem(row + j, NR)
            pltpu.make_async_remote_copy(
                src_ref=send1.at[t], dst_ref=recv1.at[row], send_sem=s1, recv_sem=r1,
                device_id={"band": in_row(t), "lev": v}, device_id_type=MESH).start()
            return 0

        lax.fori_loop(1, NR, send_1, 0)
        recv1[row] = send1[row]

    with jax.named_scope("onehot_wait"):
        coup_c.wait()
        pltpu.make_async_copy(coup_v.at[0:7], coup_v.at[0:7], rc).wait()
    with jax.named_scope("onehot"):
        lon_i = lax.broadcasted_iota(jnp.int32, (LON_W, 128), 0)

        def hot(g, _):
            for j in range(4):
                point = coup_v[g, pl.ds(j, 1), :] & (LON_W - 1)
                onehot[g * 2 + j // 2, :, (j % 2) * 128 : (j % 2) * 128 + 128] = jnp.where(
                    lon_i == point, 1.0, 0.0).astype(BF16)
            return 0

        lax.fori_loop(0, NY, hot, 0)

    with jax.named_scope("first_wait"):
        pltpu.make_async_copy(recv1.at[0 : NR - 1], recv1.at[0 : NR - 1], r1).wait()
    with jax.named_scope("repack"):
        for z in range(NZC):
            pack[z * 8 : z * 8 + 8, :] = (recv1[z] + recv1[8 + z]) + (recv1[16 + z] + recv1[24 + z])
        for j in range(NY):
            send2[j] = pack[pl.ds(j, NZC, stride=NY), :]

        def send_2(j, _):
            t = lax.rem(y + j, NY)
            pltpu.make_async_remote_copy(
                src_ref=send2.at[t], dst_ref=recv2.at[y], send_sem=s2, recv_sem=r2,
                device_id={"band": x * (NY * NZC) + t * NZC + zc, "lev": v}, device_id_type=MESH).start()
            return 0

        lax.fori_loop(1, NY, send_2, 0)
        recv2[y] = send2[y]

    with jax.named_scope("advection_wait"):
        land_c.wait()
        own_c.wait()
        for c in scalars:
            c.wait()
        halo_up.wait_recv()
        halo_down.wait_recv()
    with jax.named_scope("advection"):
        low = (lax.broadcasted_iota(jnp.int32, (half, 8, 128), 1) < 4)
        land_f = land_v[...].astype(F32)
        land8 = jnp.concatenate([land_f, land_f], axis=0)[None]
        quarter = half // 2
        tsum[...] = jnp.zeros((half, 8, 128), F32)
        first = v * (NF // NV)

        def waves(f, _):
            ext[0, :, 0:4, :] = jnp.where(b == 0, 0.0, halo[0, f].astype(F32))
            ext[0, :, 4:8, :] = own_v[f, 0:half].astype(F32)
            ext[1, :, 0:4, :] = own_v[f, half:].astype(F32)
            ext[1, :, 4:8, :] = jnp.where(b == NB - 1, 0.0, halo[1, f].astype(F32))
            speed = cour[f]
            both = []
            for side in range(2):
                parts = []
                for p in range(2):
                    span = slice(p * quarter, (p + 1) * quarter)
                    s = ext[side, span]
                    a = speed * jnp.abs(trig[0, span])
                    c = speed * trig[1, span]
                    rest = 1.0 - a - c
                    east = 1 if side == p else 127
                    north = 1 if side == 0 else 7
                    for _ in range(STEPS):
                        s = rest * s + a * pltpu.roll(s, east, 2) + c * pltpu.roll(s, north, 1)
                    parts.append(s)
                both.append(jnp.concatenate(parts, axis=0))
            s = jnp.where(low, both[1], both[0])
            energy = 1.0 + 2.0 * (first + f).astype(F32) / (NF - 1)
            tsum[...] += (energy * rate[f]) * s
            state[f] = land8 * s / (1.0 + brk[f] * s)
            return 0

        lax.fori_loop(0, NF // NV, waves, 0)

    with jax.named_scope("second_wait"):
        pltpu.make_async_copy(recv2.at[0 : NY - 1], recv2.at[0 : NY - 1], r2).wait()
    with jax.named_scope("fourier"):
        c = recv2[...].reshape(64, 128)
        lane = lax.broadcasted_iota(jnp.int32, (64, 128), 1)
        line = lax.broadcasted_iota(jnp.int32, (64, 128), 0)
        c = jnp.where((line == 0) & (lane < 6), 0.5 * c, c)
        lane = lane & 31
        field = (lane - 6 * ((lane * 43) >> 8)) >> 1
        lhs = jnp.concatenate([jnp.where(field == f, c, 0.0) for f in range(3)], axis=0).astype(BF16)
        lhs = jnp.concatenate([lhs, lhs], axis=1)
        z = jnp.dot(lhs, rhs[...], preferred_element_type=F32)
        level_weight = lw[0]
        for f in range(3):
            g = jnp.sum(
                z[64 * f : 64 * f + 64, 0:LON_W] * ebuf[0] - z[64 * f : 64 * f + 64, LON_W:] * ebuf[1],
                axis=0, keepdims=True)
            grid_o[0, 0, f : f + 1, :] = g
            if f < 2:
                for j in range(4):
                    wsend[4 * f + j : 4 * f + j + 1, :] = level_weight * g[:, 128 * j : 128 * j + 128]

    with jax.named_scope("wind_sends"):
        def send_w(j, _):
            t = lax.rem(row + j, NR)
            pltpu.make_async_remote_copy(
                src_ref=wsend, dst_ref=wrecv.at[pl.ds(pl.multiple_of(row * 8, 8), 8)], send_sem=sw, recv_sem=rw,
                device_id={"band": in_row(t), "lev": v}, device_id_type=MESH).start()
            return 0

        lax.fori_loop(1, NR, send_w, 0)
        wrecv[pl.ds(pl.multiple_of(row * 8, 8), 8), :] = wsend[...]

    with jax.named_scope("wind_wait"):
        pltpu.make_async_copy(wrecv.at[0 : 8 * NR - 8], wrecv.at[0 : 8 * NR - 8], rw).wait()
    with jax.named_scope("lookup"):
        table = jnp.concatenate(
            [
                jnp.concatenate([wrecv[pl.ds(4 * f + j, NR, stride=8), :] for j in range(4)], axis=1)
                for f in range(2)
            ],
            axis=0,
        )
        t_hi = table.astype(BF16)
    with jax.named_scope("lookup"):
        table = jnp.concatenate([t_hi, (table - t_hi.astype(F32)).astype(BF16)], axis=0)
        ri = lax.broadcasted_iota(jnp.int32, (NR, 128), 0)
        lat = (ri >> 3) * 64 + y * 8 + (ri & 7)

        def look(g, _):
            for h in range(2):
                found = jnp.dot(table, onehot[g * 2 + h], preferred_element_type=F32)
                found = found[0:64] + found[64:128]
                for j in range(2):
                    point = coup_v[g, pl.ds(2 * h + j, 1), :] >> 9
                    mine = lat == point
                    for f in range(2):
                        picked = jnp.where(mine, found[32 * f : 32 * f + 32, 128 * j : 128 * j + 128], 0.0)
                        rsend[g, pl.ds(4 * f + 2 * h + j, 1), :] = jnp.sum(picked, axis=0, keepdims=True)
            return 0

        lax.fori_loop(0, NY, look, 0)

    with jax.named_scope("sum_sends"):
        def send_r(j, _):
            g = lax.rem(col + j, NC)
            pltpu.make_async_remote_copy(
                src_ref=rsend.at[g // NV], dst_ref=rrecv.at[col], send_sem=sr, recv_sem=rr,
                device_id={"band": in_col(g), "lev": lax.rem(g, NV)}, device_id_type=MESH).start()
            return 0

        lax.fori_loop(1, NC, send_r, 0)
        rrecv[col] = rsend[y]
    with jax.named_scope("sum_wait"):
        pltpu.make_async_copy(rrecv.at[0 : NC - 1], rrecv.at[0 : NC - 1], rr).wait()
    with jax.named_scope("stress"):
        wind = jnp.sum(rrecv[...], axis=0)
        turned = pltpu.roll(wind, 4, 0)
        low8 = lax.broadcasted_iota(jnp.int32, (8, 128), 0) < 4
        east8 = jnp.where(low8, -wind, turned)
        north8 = jnp.where(low8, -turned, wind)
        push = jnp.maximum(trig[0] * east8[None] + trig[1] * north8[None], 0.0)
        stress = jnp.sum(push * tsum[...], axis=0)
        stsend[...] = stress + pltpu.roll(stress, 4, 0)

        def send_s(j, _):
            t = lax.rem(v + j, NV)
            pltpu.make_async_remote_copy(
                src_ref=stsend, dst_ref=strecv.at[v], send_sem=ss, recv_sem=rs,
                device_id={"band": b, "lev": t}, device_id_type=MESH).start()
            return 0

        lax.fori_loop(1, NV, send_s, 0)
        strecv[v] = stsend[...]

    with jax.named_scope("result"):
        def result(f, _):
            s = state[f]
            s = s + s * (rate[f] * push)
            res[f, 0:half] = s[:, 4:8, :]
            res[f, half:] = s[:, 0:4, :]
            return 0

        lax.fori_loop(0, NF // NV, result, 0)
        out_c = pltpu.make_async_copy(res, out_o, out_s)
        out_c.start()

    with jax.named_scope("stress_wait"):
        pltpu.make_async_copy(strecv.at[0 : NV - 1], strecv.at[0 : NV - 1], rs).wait()
    with jax.named_scope("charnock"):
        total = (strecv[0] + strecv[1]) + (strecv[2] + strecv[3])
        mean = total * land8[0] * (1.0 / (NF * ND))
        charnock = 0.011 + 0.5 * mean / (mean + 0.05 * (1.0 + wind * wind + turned * turned))
        char_o[...] = charnock[0:4]

    with jax.named_scope("drain"):
        halo_up.wait_send()
        halo_down.wait_send()
        pltpu.make_async_copy(coup_v.at[0:7], coup_v.at[0:7], sc).wait()
        pltpu.make_async_copy(send1.at[0 : NR - 1], send1.at[0 : NR - 1], s1).wait()
        pltpu.make_async_copy(send2.at[0 : NY - 1], send2.at[0 : NY - 1], s2).wait()
        pltpu.make_async_copy(wrecv.at[0 : 8 * NR - 8], wrecv.at[0 : 8 * NR - 8], sw).wait()
        pltpu.make_async_copy(rrecv.at[0 : NC - 1], rrecv.at[0 : NC - 1], sr).wait()
        pltpu.make_async_copy(strecv.at[0 : NV - 1], strecv.at[0 : NV - 1], ss).wait()
        out_c.wait()


def on_device(spectral, legendre, level_weights, coupling, land_sea, spectra, courant, growth_rate, breaking):
    spec = jnp.transpose(spectral, (0, 2, 3, 1, 4)).reshape(15, 2, N)
    any_, vm = (pl.BlockSpec(memory_space=s) for s in (pl.ANY, pltpu.VMEM))
    sm = pltpu.SMEM
    dma = pltpu.SemaphoreType.DMA
    nf, half = NF // NV, ND // 2
    return pl.pallas_call(
        kernel,
        out_shape=(
            jax.ShapeDtypeStruct((1, 1, 3, LON_W), F32),
            jax.ShapeDtypeStruct((nf, ND, 4, 128), F32),
            jax.ShapeDtypeStruct((4, 128), F32),
        ),
        in_specs=[any_, any_, pl.BlockSpec(memory_space=sm)] + [any_] * 6,
        out_specs=(vm, any_, vm),
        scratch_shapes=[
            pltpu.VMEM((5, NLAT, N), BF16),
            pltpu.VMEM((15, 2, N), BF16),
            pltpu.VMEM((NY, 4, 128), jnp.int32),
            pltpu.VMEM((4, 128), jnp.int32),
            pltpu.VMEM((nf, ND, 4, 128), BF16),
            pltpu.VMEM((32, N), F32),
            pltpu.VMEM((NLAT, 128), F32),
            pltpu.VMEM((NR, 8, 128), F32),
            pltpu.VMEM((NR, 8, 128), F32),
            pltpu.VMEM((64, 128), F32),
            pltpu.VMEM((NY, 8, 128), F32),
            pltpu.VMEM((NY, 8, 128), F32),
            pltpu.VMEM((256, 2 * LON_W), BF16),
            pltpu.VMEM((2, 64, LON_W), F32),
            pltpu.VMEM((8, 128), F32),
            pltpu.VMEM((8 * NR, 128), F32),
            pltpu.VMEM((2 * NY, LON_W, 256), BF16),
            pltpu.VMEM((NY, 8, 128), F32),
            pltpu.VMEM((NC, 8, 128), F32),
            pltpu.VMEM((2, nf, half, 4, 128), BF16),
            pltpu.VMEM((2, half, 8, 128), F32),
            pltpu.VMEM((2, half, 8, 128), F32),
            pltpu.VMEM((nf, half, 8, 128), F32),
            pltpu.VMEM((half, 8, 128), F32),
            pltpu.VMEM((8, 128), F32),
            pltpu.VMEM((NV, 8, 128), F32),
            pltpu.VMEM((nf, ND, 4, 128), F32),
            sm((nf,), F32), sm((nf,), F32), sm((nf,), F32),
            dma((5,)), dma((8,)), dma,
            dma, dma, dma, dma, dma, dma, dma, dma,
            dma((2,)), dma((2,)), dma, dma, dma, dma,
        ],
        compiler_params=pltpu.CompilerParams(
            collective_id=0, has_side_effects=True, vmem_limit_bytes=56 * 1024 * 1024
        ),
    )(spec, legendre, level_weights, coupling, land_sea, spectra, courant, growth_rate, breaking)


def solution(mesh):
    in_specs = (
        P("band", None, "lev", None, None),
        P("band", None, None),
        P("lev"),
        P("band", None),
        P("band", None),
        P("lev", None, "band", None),
        P("lev"),
        P("lev"),
        P("lev"),
    )
    out_specs = (P("band", "lev", None, None), P("lev", None, "band", None), P("band", None))
    return jax.shard_map(on_device, mesh=mesh, in_specs=in_specs, out_specs=out_specs, check_vma=False)
```

```python
import math

import jax
import jax.numpy as jnp
from jax import lax
from jax.experimental import pallas as pl
from jax.experimental.pallas import tpu as pltpu
from jax.sharding import PartitionSpec as P

N = 1280
NLON = 5136
LON_W = 512
NLAT = 256
NF = 36
ND = 36
STEPS = 4
NX, NY, NZC, NV = 4, 8, 8, 4
NB = NX * NY * NZC
NXY = NX * NY
NZ = NV * NZC
HALF = ND // 2
MESH = pl.DeviceIdType.MESH
F32, BF16 = jnp.float32, jnp.bfloat16


def turn(t):
    u = (t - jnp.floor(t + 0.5)) * (2.0 * math.pi)
    s = u * u
    even = jnp.full_like(u, 1.0 / math.factorial(16))
    odd = jnp.full_like(u, -1.0 / math.factorial(17 - 2))
    for k in range(7, -1, -1):
        even = even * s + (-1.0) ** k / math.factorial(2 * k)
        if k < 7:
            odd = odd * s + (-1.0) ** k / math.factorial(2 * k + 1)
    return even, u * odd


def cycles(product):
    return (product - jnp.floor(product * (1.0 / NLON)) * NLON) * (1.0 / NLON)


def plane_offset(x, y, j):
    dy = lax.rem(NY // 2 + ring(j // NX, NY), NY)
    dx = lax.rem(NX // 2 + ring(lax.rem(j, NX), NX), NX)
    return lax.rem(x + dx, NX) * NY + lax.rem(y + dy, NY)


def line_offset(z, j):
    return lax.rem(z + NZ // 2 + ring(j, NZ), NZ)


def ring(j, n):
    k = (j + 1) // 2
    return lax.rem(n + k * (2 * lax.rem(j, 2) - 1), n)


def kernel(
    lw, spec, leg, coup, land, spectra, cour_h, rate_h, brk_h,
    grid_o, out_o, char_o,
    leg_v, spec_v, coup_v, land_v, own_v, s32, proj, recv1, pack, send2, recv2,
    rhs, ebuf, wsend, wrecv, onehot, rsend, rrecv, halo, ext, trig, state, tsum, tsend, trecv,
    cour, rate, brk,
    leg_s, in_s, s1, r1, s2, r2, sw, rw, sr, rr, sh, rh, sc, rc, ss, rs,
):
    b = lax.axis_index("band")
    v = lax.axis_index("lev")
    xy = b // NZC
    x = xy // NY
    y = lax.rem(xy, NY)
    zc = lax.rem(b, NZC)
    zp = v * NZC + zc
    up = lax.rem(b + 1, NB)
    down = lax.rem(b + NB - 1, NB)

    loads = [pltpu.make_async_copy(leg.at[m], leg_v.at[m], leg_s.at[m]) for m in range(5)]
    spec_c = pltpu.make_async_copy(spec, spec_v, in_s.at[0])
    coup_c = pltpu.make_async_copy(coup, coup_v.at[zc], in_s.at[1])
    land_c = pltpu.make_async_copy(land, land_v, in_s.at[2])
    own_c = pltpu.make_async_copy(spectra, own_v, in_s.at[3])
    scalars = [
        pltpu.make_async_copy(h, t, in_s.at[4 + i])
        for i, (h, t) in enumerate(((cour_h, cour), (rate_h, rate), (brk_h, brk)))
    ]
    spec_c.start()
    for c in (*loads, coup_c, land_c, own_c, *scalars):
        c.start()

    barrier = pltpu.get_barrier_semaphore()

    def greet_plane(j, _):
        t = plane_offset(x, y, j)
        pl.semaphore_signal(barrier, inc=1, device_id={"band": t * NZC + zc, "lev": v}, device_id_type=MESH)
        return 0

    def greet_line(j, _):
        t = lax.rem(zp + j, NZ)
        pl.semaphore_signal(
            barrier, inc=1, device_id={"band": xy * NZC + lax.rem(t, NZC), "lev": t // NZC},
            device_id_type=MESH)
        return 0

    lax.fori_loop(0, NXY - 1, greet_plane, 0)
    lax.fori_loop(1, NZ, greet_line, 0)
    pl.semaphore_signal(barrier, inc=1, device_id={"band": up, "lev": v}, device_id_type=MESH)
    pl.semaphore_signal(barrier, inc=1, device_id={"band": down, "lev": v}, device_id_type=MESH)

    spec_c.wait()
    s32[30:32, :] = jnp.zeros((2, N), F32)
    for j in range(15):
        s32[2 * j : 2 * j + 2, :] = spec_v[j].astype(F32)
    sl = lax.broadcasted_iota(jnp.int32, (128, N), 0)
    held = s32[...]
    held = jnp.concatenate([held, held, held, held], axis=0)
    sm = ((sl & 31) * 43) >> 8
    held = jnp.where((sl >> 5) == x, held, 0.0)
    acc = None
    for m in range(5):
        s_m = jnp.where(sm == m, held, 0.0).astype(BF16)
        loads[m].wait()
        d = lax.dot_general(leg_v[m], s_m, (((1,), (1,)), ((), ())), preferred_element_type=F32)
        acc = d if acc is None else acc + d
    proj[...] = acc.astype(BF16).astype(F32).reshape(NXY, 8, 128)

    pl.semaphore_wait(barrier, NXY - 1 + NZ - 1 + 2)

    def send_1(j, _):
        t = plane_offset(x, y, j)
        pltpu.make_async_remote_copy(
            src_ref=proj.at[t], dst_ref=recv1.at[xy], send_sem=s1, recv_sem=r1,
            device_id={"band": t * NZC + zc, "lev": v}, device_id_type=MESH).start()
        return 0

    lax.fori_loop(0, NXY - 1, send_1, 0)
    recv1[xy] = proj[xy]

    halo_up = pltpu.make_async_remote_copy(
        src_ref=spectra.at[:, 0:HALF], dst_ref=halo.at[0], send_sem=sh.at[0], recv_sem=rh.at[0],
        device_id={"band": up, "lev": v}, device_id_type=MESH)
    halo_down = pltpu.make_async_remote_copy(
        src_ref=spectra.at[:, HALF:], dst_ref=halo.at[1], send_sem=sh.at[1], recv_sem=rh.at[1],
        device_id={"band": down, "lev": v}, device_id_type=MESH)

    def send_coup(j, _):
        t = lax.rem(zc + j, NZC)
        pltpu.make_async_remote_copy(
            src_ref=coup, dst_ref=coup_v.at[zc], send_sem=sc, recv_sem=rc,
            device_id={"band": xy * NZC + t, "lev": v}, device_id_type=MESH).start()
        return 0

    lax.fori_loop(1, NZC, send_coup, 0)
    halo_up.start()
    halo_down.start()

    slot = lax.broadcasted_iota(jnp.int32, (128, LON_W), 0)
    lon = lax.broadcasted_iota(jnp.int32, (128, LON_W), 1).astype(F32)
    xs = slot >> 5
    slot = slot & 31
    mi = (slot * 43) >> 8
    k = (xs * 320 + mi).astype(F32)
    part = (slot & 1).astype(F32)
    re, im = turn(cycles(k * lon) + 0.25 * part)
    re_hi, im_hi = re.astype(BF16), im.astype(BF16)
    rhs[0:128, 0:LON_W] = re_hi
    rhs[0:128, LON_W:] = im_hi
    rhs[128:256, 0:LON_W] = (re - re_hi.astype(F32)).astype(BF16)
    rhs[128:256, LON_W:] = (im - im_hi.astype(F32)).astype(BF16)
    q = lax.broadcasted_iota(jnp.int32, (64, LON_W), 0)
    q = ((q & 7) * 8 + (q >> 3)).astype(F32)
    lon = lax.broadcasted_iota(jnp.int32, (64, LON_W), 1).astype(F32)
    ec, es = turn(cycles(q * 5.0 * lon))
    ebuf[0] = 2.0 * ec
    ebuf[1] = 2.0 * es
    e = lax.broadcasted_iota(jnp.int32, (HALF, 8, 128), 0).astype(F32)
    tc, ts = turn((e + 0.5) * (1.0 / ND))
    trig[0] = tc
    trig[1] = ts

    coup_c.wait()
    pltpu.make_async_copy(coup_v.at[0:7], coup_v.at[0:7], rc).wait()
    lon_i = lax.broadcasted_iota(jnp.int32, (LON_W, 128), 0)

    def hot(g, _):
        for j in range(4):
            point = coup_v[g, pl.ds(j, 1), :] & (LON_W - 1)
            onehot[g * 2 + j // 2, :, (j % 2) * 128 : (j % 2) * 128 + 128] = jnp.where(
                lon_i == point, 1.0, 0.0).astype(BF16)
        return 0

    lax.fori_loop(0, NZC, hot, 0)

    pltpu.make_async_copy(recv1.at[0 : NXY - 1], recv1.at[0 : NXY - 1], r1).wait()
    for j in range(NY):
        pack[j * 8 : j * 8 + 8, :] = (recv1[j] + recv1[8 + j]) + (recv1[16 + j] + recv1[24 + j])
    for j in range(NZC):
        send2[j] = pack[pl.ds(j, NY, stride=NZC), :]

    def send_2(j, _):
        t = lax.rem(zc + j, NZC)
        pltpu.make_async_remote_copy(
            src_ref=send2.at[t], dst_ref=recv2.at[zc], send_sem=s2, recv_sem=r2,
            device_id={"band": xy * NZC + t, "lev": v}, device_id_type=MESH).start()
        return 0

    lax.fori_loop(1, NZC, send_2, 0)
    recv2[zc] = send2[zc]

    land_c.wait()
    own_c.wait()
    for c in scalars:
        c.wait()
    halo_up.wait_recv()
    halo_down.wait_recv()
    low = lax.broadcasted_iota(jnp.int32, (HALF, 8, 128), 1) < 4
    land_f = land_v[...].astype(F32)
    land8 = jnp.concatenate([land_f, land_f], axis=0)[None]
    quarter = HALF // 2
    tsum[...] = jnp.zeros((HALF, 8, 128), F32)
    first = v * (NF // NV)

    def waves(f, _):
        ext[0, :, 0:4, :] = jnp.where(b == 0, 0.0, halo[0, f].astype(F32))
        ext[0, :, 4:8, :] = own_v[f, 0:HALF].astype(F32)
        ext[1, :, 0:4, :] = own_v[f, HALF:].astype(F32)
        ext[1, :, 4:8, :] = jnp.where(b == NB - 1, 0.0, halo[1, f].astype(F32))
        speed = cour[f]
        both = []
        for side in range(2):
            parts = []
            for p in range(2):
                span = slice(p * quarter, (p + 1) * quarter)
                s = ext[side, span]
                a = speed * jnp.abs(trig[0, span])
                c = speed * trig[1, span]
                rest = 1.0 - a - c
                east = 1 if side == p else 127
                north = 1 if side == 0 else 7
                for _ in range(STEPS):
                    s = rest * s + a * pltpu.roll(s, east, 2) + c * pltpu.roll(s, north, 1)
                parts.append(s)
            both.append(jnp.concatenate(parts, axis=0))
        s = jnp.where(low, both[1], both[0])
        energy = 1.0 + 2.0 * (first + f).astype(F32) / (NF - 1)
        tsum[...] += (energy * rate[f]) * s
        state[f] = land8 * s / (1.0 + brk[f] * s)
        return 0

    lax.fori_loop(0, NF // NV, waves, 0)
    tsend[...] = tsum[...].reshape(HALF * 8, 128).astype(BF16)

    def send_t(j, _):
        t = lax.rem(v + j, NV)
        pltpu.make_async_remote_copy(
            src_ref=tsend, dst_ref=trecv.at[v], send_sem=ss, recv_sem=rs,
            device_id={"band": b, "lev": t}, device_id_type=MESH).start()
        return 0

    lax.fori_loop(1, NV, send_t, 0)

    pltpu.make_async_copy(recv2.at[0 : NZC - 1], recv2.at[0 : NZC - 1], r2).wait()
    c = recv2[...].reshape(64, 128)
    lane = lax.broadcasted_iota(jnp.int32, (64, 128), 1)
    row = lax.broadcasted_iota(jnp.int32, (64, 128), 0)
    c = jnp.where((row == 0) & (lane < 6), 0.5 * c, c)
    lane = lane & 31
    field = (lane - 6 * ((lane * 43) >> 8)) >> 1
    lhs = jnp.concatenate([jnp.where(field == f, c, 0.0) for f in range(3)], axis=0).astype(BF16)
    lhs = jnp.concatenate([lhs, lhs], axis=1)
    z = jnp.dot(lhs, rhs[...], preferred_element_type=F32)
    level_weight = lw[0]
    for f in range(3):
        g = jnp.sum(
            z[64 * f : 64 * f + 64, 0:LON_W] * ebuf[0] - z[64 * f : 64 * f + 64, LON_W:] * ebuf[1],
            axis=0, keepdims=True)
        grid_o[0, f] = g
        if f < 2:
            for j in range(4):
                wsend[4 * f + j : 4 * f + j + 1, :] = level_weight * g[:, 128 * j : 128 * j + 128]

    def send_w(j, _):
        t = plane_offset(x, y, j)
        pltpu.make_async_remote_copy(
            src_ref=wsend, dst_ref=wrecv.at[pl.ds(pl.multiple_of(xy * 8, 8), 8)], send_sem=sw, recv_sem=rw,
            device_id={"band": t * NZC + zc, "lev": v}, device_id_type=MESH).start()
        return 0

    lax.fori_loop(0, NXY - 1, send_w, 0)
    wrecv[pl.ds(pl.multiple_of(xy * 8, 8), 8), :] = wsend[...]

    pltpu.make_async_copy(wrecv.at[0 : 8 * NXY - 8], wrecv.at[0 : 8 * NXY - 8], rw).wait()
    table = jnp.concatenate(
        [
            jnp.concatenate([wrecv[pl.ds(4 * f + j, NXY, stride=8), :] for j in range(4)], axis=1)
            for f in range(2)
        ],
        axis=0,
    )
    t_hi = table.astype(BF16)
    table = jnp.concatenate([t_hi, (table - t_hi.astype(F32)).astype(BF16)], axis=0)
    lat = lax.broadcasted_iota(jnp.int32, (NXY, 128), 0) * NZC + zc

    def look(g, _):
        for h in range(2):
            found = jnp.dot(table, onehot[g * 2 + h], preferred_element_type=F32)
            found = found[0:64] + found[64:128]
            for j in range(2):
                point = coup_v[g, pl.ds(2 * h + j, 1), :] >> 9
                mine = lat == point
                for f in range(2):
                    picked = jnp.where(mine, found[32 * f : 32 * f + 32, 128 * j : 128 * j + 128], 0.0)
                    rsend[g, pl.ds(4 * f + 2 * h + j, 1), :] = jnp.sum(picked, axis=0, keepdims=True)
        return 0

    lax.fori_loop(0, NZC, look, 0)

    def send_r(j, _):
        t = line_offset(zp, j)
        g = lax.rem(t, NZC)
        pltpu.make_async_remote_copy(
            src_ref=rsend.at[g], dst_ref=rrecv.at[zp], send_sem=sr, recv_sem=rr,
            device_id={"band": xy * NZC + g, "lev": t // NZC}, device_id_type=MESH).start()
        return 0

    lax.fori_loop(0, NZ - 1, send_r, 0)
    rrecv[zp] = rsend[zc]

    pltpu.make_async_copy(trecv.at[0 : NV - 1], trecv.at[0 : NV - 1], rs).wait()
    total = tsum[...]
    for j in range(1, NV):
        total = total + trecv[lax.rem(v + j, NV)].astype(F32).reshape(HALF, 8, 128)
    tsum[...] = total

    pltpu.make_async_copy(rrecv.at[0 : NZ - 1], rrecv.at[0 : NZ - 1], rr).wait()
    wind = jnp.sum(rrecv[...], axis=0)
    turned = pltpu.roll(wind, 4, 0)
    low8 = lax.broadcasted_iota(jnp.int32, (8, 128), 0) < 4
    east8 = jnp.where(low8, -wind, turned)
    north8 = jnp.where(low8, -turned, wind)
    push = jnp.maximum(trig[0] * east8[None] + trig[1] * north8[None], 0.0)
    stress = jnp.sum(push * tsum[...], axis=0)
    mean = (stress + pltpu.roll(stress, 4, 0)) * land8[0] * (1.0 / (NF * ND))
    charnock = 0.011 + 0.5 * mean / (mean + 0.05 * (1.0 + wind * wind + turned * turned))
    char_o[...] = charnock[0:4]

    def result(f, _):
        s = state[f]
        s = s + s * (rate[f] * push)
        out_o[f, 0:HALF] = s[:, 4:8, :]
        out_o[f, HALF:] = s[:, 0:4, :]
        return 0

    lax.fori_loop(0, NF // NV, result, 0)

    halo_up.wait_send()
    halo_down.wait_send()
    pltpu.make_async_copy(coup_v.at[0:7], coup_v.at[0:7], sc).wait()
    pltpu.make_async_copy(recv1.at[0 : NXY - 1], recv1.at[0 : NXY - 1], s1).wait()
    pltpu.make_async_copy(send2.at[0 : NZC - 1], send2.at[0 : NZC - 1], s2).wait()
    pltpu.make_async_copy(wrecv.at[0 : 8 * NXY - 8], wrecv.at[0 : 8 * NXY - 8], sw).wait()
    pltpu.make_async_copy(rrecv.at[0 : NZ - 1], rrecv.at[0 : NZ - 1], sr).wait()
    pltpu.make_async_copy(trecv.at[0 : NV - 1], trecv.at[0 : NV - 1], ss).wait()


def write(grid, out, char, grid_o, out_o, char_o, sems):
    copies = [
        pltpu.make_async_copy(s, d, sems.at[i])
        for i, (s, d) in enumerate(((out, out_o), (grid, grid_o), (char, char_o)))
    ]
    for c in copies:
        c.start()
    for c in copies:
        c.wait()


def on_device(spectral, legendre, level_weights, coupling, land_sea, spectra, courant, growth_rate, breaking):
    spec = jnp.transpose(spectral, (0, 2, 3, 1, 4)).reshape(15, 2, N)
    hbm, vm = (pl.BlockSpec(memory_space=s) for s in (pltpu.HBM, pltpu.VMEM))
    sm = pltpu.SMEM
    dma = pltpu.SemaphoreType.DMA
    nf = NF // NV
    shapes = (
        jax.ShapeDtypeStruct((1, 3, 1, LON_W), F32),
        jax.ShapeDtypeStruct((nf, ND, 4, 128), F32),
        jax.ShapeDtypeStruct((4, 128), F32),
    )
    grid, out, char = pl.pallas_call(
        kernel,
        out_shape=shapes,
        in_specs=[pl.BlockSpec(memory_space=sm)] + [hbm] * 8,
        out_specs=(vm, vm, vm),
        scratch_shapes=[
            pltpu.VMEM((5, NLAT, N), BF16),
            pltpu.VMEM((15, 2, N), BF16),
            pltpu.VMEM((NZC, 4, 128), jnp.int32),
            pltpu.VMEM((4, 128), jnp.int32),
            pltpu.VMEM((nf, ND, 4, 128), BF16),
            pltpu.VMEM((32, N), F32),
            pltpu.VMEM((NXY, 8, 128), F32),
            pltpu.VMEM((NXY, 8, 128), F32),
            pltpu.VMEM((64, 128), F32),
            pltpu.VMEM((NZC, 8, 128), F32),
            pltpu.VMEM((NZC, 8, 128), F32),
            pltpu.VMEM((256, 2 * LON_W), BF16),
            pltpu.VMEM((2, 64, LON_W), F32),
            pltpu.VMEM((8, 128), F32),
            pltpu.VMEM((8 * NXY, 128), F32),
            pltpu.VMEM((2 * NZC, LON_W, 256), BF16),
            pltpu.VMEM((NZC, 8, 128), F32),
            pltpu.VMEM((NZ, 8, 128), F32),
            pltpu.VMEM((2, nf, HALF, 4, 128), BF16),
            pltpu.VMEM((2, HALF, 8, 128), F32),
            pltpu.VMEM((2, HALF, 8, 128), F32),
            pltpu.VMEM((nf, HALF, 8, 128), F32),
            pltpu.VMEM((HALF, 8, 128), F32),
            pltpu.VMEM((HALF * 8, 128), BF16),
            pltpu.VMEM((NV, HALF * 8, 128), BF16),
            sm((nf,), F32), sm((nf,), F32), sm((nf,), F32),
            dma((5,)), dma((8,)),
            dma, dma, dma, dma, dma, dma, dma, dma,
            dma((2,)), dma((2,)), dma, dma, dma, dma,
        ],
        compiler_params=pltpu.CompilerParams(
            collective_id=0, has_side_effects=True, vmem_limit_bytes=40 * 1024 * 1024
        ),
    )(
        level_weights,
        *(
            pltpu.with_memory_space_constraint(a, pltpu.HBM)
            for a in (spec, legendre, coupling, land_sea, spectra, courant, growth_rate, breaking)
        ),
    )
    grid, out, char = pl.pallas_call(
        write,
        out_shape=shapes,
        in_specs=[vm] * 3,
        out_specs=[hbm] * 3,
        scratch_shapes=[dma((3,))],
        compiler_params=pltpu.CompilerParams(vmem_limit_bytes=16 * 1024 * 1024),
    )(grid, out, char)
    return jnp.transpose(grid, (0, 2, 1, 3)), out, char


def solution(mesh):
    in_specs = (
        P("band", None, "lev", None, None),
        P("band", None, None),
        P("lev"),
        P("band", None),
        P("band", None),
        P("lev", None, "band", None),
        P("lev"),
        P("lev"),
        P("lev"),
    )
    out_specs = (P("band", "lev", None, None), P("lev", None, "band", None), P("band", None))
    return jax.shard_map(on_device, mesh=mesh, in_specs=in_specs, out_specs=out_specs, check_vma=False)
```

```python
import math

import jax
import jax.numpy as jnp
from jax import lax
from jax.experimental import pallas as pl
from jax.experimental.pallas import tpu as pltpu
from jax.sharding import PartitionSpec as P

N = 1280
NLON = 5136
LON_W = 512
NLAT = 256
NF = 36
ND = 36
STEPS = 4
NX, NY, NZC, NV = 4, 8, 8, 4
NB = NX * NY * NZC
NXY = NX * NY
NZ = NV * NZC
HALF = ND // 2
MESH = pl.DeviceIdType.MESH
F32, BF16 = jnp.float32, jnp.bfloat16


def turn(t):
    u = (t - jnp.floor(t + 0.5)) * (2.0 * math.pi)
    s = u * u
    even = jnp.full_like(u, 1.0 / math.factorial(16))
    odd = jnp.full_like(u, -1.0 / math.factorial(17 - 2))
    for k in range(7, -1, -1):
        even = even * s + (-1.0) ** k / math.factorial(2 * k)
        if k < 7:
            odd = odd * s + (-1.0) ** k / math.factorial(2 * k + 1)
    return even, u * odd


def cycles(product):
    return (product - jnp.floor(product * (1.0 / NLON)) * NLON) * (1.0 / NLON)


def plane_partners(x, y):
    xs = [lax.rem(x + d, NX) * NY for d in (2, 3, 1, 0)]
    for dy in (4, 5, 3, 6, 2, 7, 1, 0):
        yy = lax.rem(y + dy, NY)
        for xx in xs[: 4 if dy else 3]:
            yield xx + yy


def line_partners(v, zc):
    vs = [lax.rem(v + d, NV) for d in (2, 1, 3, 0)]
    zs = [lax.rem(zc + d, NZC) for d in range(NZC)]
    for i, vv in enumerate(vs):
        for zz in zs[1 if i == 3 else 0 :]:
            yield vv, zz


def kernel(
    lw, spec, leg, coup, land, spectra, cour_h, rate_h, brk_h,
    grid_o, out_o, char_o,
    leg_v, spec_v, coup_v, land_v, own_v, s32, proj, recv1, pack, send2, recv2,
    rhs, ebuf, wrow, wsend, wrecv, wtab, onehot, rrow, rsend, rrecv, halo, ext, trig, state, tsum, tsend, trecv,
    cour, rate, brk,
    leg_s, in_s, s1, r1, s2, r2, sw, rw, sr, rr, sh, rh, sc, rc, ss, rs,
):
    b = lax.axis_index("band")
    v = lax.axis_index("lev")
    xy = b // NZC
    x = xy // NY
    y = lax.rem(xy, NY)
    zc = lax.rem(b, NZC)
    zp = v * NZC + zc
    up = lax.rem(b + 1, NB)
    down = lax.rem(b + NB - 1, NB)

    loads = [pltpu.make_async_copy(leg.at[m], leg_v.at[m], leg_s.at[m]) for m in range(5)]
    spec_c = pltpu.make_async_copy(spec, spec_v, in_s.at[0])
    coup_c = pltpu.make_async_copy(coup, coup_v.at[zc], in_s.at[1])
    land_c = pltpu.make_async_copy(land, land_v, in_s.at[2])
    own_c = pltpu.make_async_copy(spectra, own_v, in_s.at[3])
    scalars = [
        pltpu.make_async_copy(h, t, in_s.at[4 + i])
        for i, (h, t) in enumerate(((cour_h, cour), (rate_h, rate), (brk_h, brk)))
    ]
    spec_c.start()
    for c in (*loads, coup_c, land_c, own_c, *scalars):
        c.start()

    barrier = pltpu.get_barrier_semaphore()

    for vv, zz in line_partners(v, zc):
        pl.semaphore_signal(
            barrier, inc=1, device_id={"band": xy * NZC + zz, "lev": vv}, device_id_type=MESH)
    for t in plane_partners(x, y):
        pl.semaphore_signal(barrier, inc=1, device_id={"band": t * NZC + zc, "lev": v}, device_id_type=MESH)
    pl.semaphore_signal(barrier, inc=1, device_id={"band": up, "lev": v}, device_id_type=MESH)
    pl.semaphore_signal(barrier, inc=1, device_id={"band": down, "lev": v}, device_id_type=MESH)

    spec_c.wait()
    s32[30:32, :] = jnp.zeros((2, N), F32)
    for j in range(15):
        s32[2 * j : 2 * j + 2, :] = spec_v[j].astype(F32)
    sl = lax.broadcasted_iota(jnp.int32, (128, N), 0)
    held = s32[...]
    held = jnp.concatenate([held, held, held, held], axis=0)
    sm = ((sl & 31) * 43) >> 8
    held = jnp.where((sl >> 5) == x, held, 0.0)
    acc = None
    for m in range(5):
        s_m = jnp.where(sm == m, held, 0.0).astype(BF16)
        loads[m].wait()
        d = lax.dot_general(leg_v[m], s_m, (((1,), (1,)), ((), ())), preferred_element_type=F32)
        acc = d if acc is None else acc + d
    proj[...] = acc.reshape(NXY, 8, 128).astype(BF16)

    pl.semaphore_wait(barrier, NXY - 1 + NZ - 1 + 2)

    for t in plane_partners(x, y):
        pltpu.make_async_remote_copy(
            src_ref=proj.at[t], dst_ref=recv1.at[xy], send_sem=s1, recv_sem=r1,
            device_id={"band": t * NZC + zc, "lev": v}, device_id_type=MESH).start()
    recv1[xy] = proj[xy]

    halo_up = pltpu.make_async_remote_copy(
        src_ref=spectra.at[:, 0:HALF], dst_ref=halo.at[0], send_sem=sh.at[0], recv_sem=rh.at[0],
        device_id={"band": up, "lev": v}, device_id_type=MESH)
    halo_down = pltpu.make_async_remote_copy(
        src_ref=spectra.at[:, HALF:], dst_ref=halo.at[1], send_sem=sh.at[1], recv_sem=rh.at[1],
        device_id={"band": down, "lev": v}, device_id_type=MESH)

    def send_coup(j, _):
        t = lax.rem(zc + j, NZC)
        pltpu.make_async_remote_copy(
            src_ref=coup, dst_ref=coup_v.at[zc], send_sem=sc, recv_sem=rc,
            device_id={"band": xy * NZC + t, "lev": v}, device_id_type=MESH).start()
        return 0

    lax.fori_loop(1, NZC, send_coup, 0)
    halo_up.start()
    halo_down.start()

    slot = lax.broadcasted_iota(jnp.int32, (128, LON_W), 0)
    lon = lax.broadcasted_iota(jnp.int32, (128, LON_W), 1).astype(F32)
    xs = slot >> 5
    slot = slot & 31
    mi = (slot * 43) >> 8
    k = (xs * 320 + mi).astype(F32)
    part = (slot & 1).astype(F32)
    re, im = turn(cycles(k * lon) + 0.25 * part)
    re_hi, im_hi = re.astype(BF16), im.astype(BF16)
    rhs[0:128, 0:LON_W] = re_hi
    rhs[0:128, LON_W:] = im_hi
    rhs[128:256, 0:LON_W] = (re - re_hi.astype(F32)).astype(BF16)
    rhs[128:256, LON_W:] = (im - im_hi.astype(F32)).astype(BF16)
    q = lax.broadcasted_iota(jnp.int32, (64, LON_W), 0)
    q = ((q & 7) * 8 + (q >> 3)).astype(F32)
    lon = lax.broadcasted_iota(jnp.int32, (64, LON_W), 1).astype(F32)
    ec, es = turn(cycles(q * 5.0 * lon))
    ebuf[0] = 2.0 * ec
    ebuf[1] = 2.0 * es
    e = lax.broadcasted_iota(jnp.int32, (HALF, 8, 128), 0).astype(F32)
    tc, ts = turn((e + 0.5) * (1.0 / ND))
    trig[0] = tc
    trig[1] = ts

    coup_c.wait()
    pltpu.make_async_copy(coup_v.at[0:7], coup_v.at[0:7], rc).wait()
    lon_i = lax.broadcasted_iota(jnp.int32, (LON_W, 128), 0)

    def hot(g, _):
        for j in range(4):
            point = coup_v[g, pl.ds(j, 1), :] & (LON_W - 1)
            onehot[g * 2 + j // 2, :, (j % 2) * 128 : (j % 2) * 128 + 128] = jnp.where(
                lon_i == point, 1.0, 0.0).astype(BF16)
        return 0

    lax.fori_loop(0, NZC, hot, 0)

    pltpu.make_async_copy(recv1.at[0 : NXY - 1], recv1.at[0 : NXY - 1], r1).wait()
    for j in range(NY):
        parts = [recv1[8 * i + j].astype(F32) for i in range(NX)]
        pack[j * 8 : j * 8 + 8, :] = (parts[0] + parts[1]) + (parts[2] + parts[3])
    for j in range(NZC):
        send2[j] = pack[pl.ds(j, NY, stride=NZC), :].astype(BF16)

    for j in (4, 3, 5, 2, 6, 1, 7):
        t = lax.rem(zc + j, NZC)
        pltpu.make_async_remote_copy(
            src_ref=send2.at[t], dst_ref=recv2.at[zc], send_sem=s2, recv_sem=r2,
            device_id={"band": xy * NZC + t, "lev": v}, device_id_type=MESH).start()
    recv2[zc] = send2[zc]

    land_c.wait()
    own_c.wait()
    for c in scalars:
        c.wait()
    halo_up.wait_recv()
    halo_down.wait_recv()
    low = lax.broadcasted_iota(jnp.int32, (HALF, 8, 128), 1) < 4
    land_f = land_v[...].astype(F32)
    land8 = jnp.concatenate([land_f, land_f], axis=0)[None]
    quarter = HALF // 2
    tsum[...] = jnp.zeros((HALF, 8, 128), F32)
    first = v * (NF // NV)

    def waves(f, _):
        ext[0, :, 0:4, :] = jnp.where(b == 0, 0.0, halo[0, f].astype(F32))
        ext[0, :, 4:8, :] = own_v[f, 0:HALF].astype(F32)
        ext[1, :, 0:4, :] = own_v[f, HALF:].astype(F32)
        ext[1, :, 4:8, :] = jnp.where(b == NB - 1, 0.0, halo[1, f].astype(F32))
        speed = cour[f]
        both = []
        for side in range(2):
            parts = []
            for p in range(2):
                span = slice(p * quarter, (p + 1) * quarter)
                s = ext[side, span]
                a = speed * jnp.abs(trig[0, span])
                c = speed * trig[1, span]
                rest = 1.0 - a - c
                east = 1 if side == p else 127
                north = 1 if side == 0 else 7
                for _ in range(STEPS):
                    s = rest * s + a * pltpu.roll(s, east, 2) + c * pltpu.roll(s, north, 1)
                parts.append(s)
            both.append(jnp.concatenate(parts, axis=0))
        s = jnp.where(low, both[1], both[0])
        energy = 1.0 + 2.0 * (first + f).astype(F32) / (NF - 1)
        tsum[...] += (energy * rate[f]) * s
        state[f] = land8 * s / (1.0 + brk[f] * s)
        return 0

    lax.fori_loop(0, NF // NV, waves, 0)
    tsend[...] = tsum[...].reshape(HALF * 8, 128).astype(BF16)

    def send_t(j, _):
        t = lax.rem(v + j, NV)
        pltpu.make_async_remote_copy(
            src_ref=tsend, dst_ref=trecv.at[v], send_sem=ss, recv_sem=rs,
            device_id={"band": b, "lev": t}, device_id_type=MESH).start()
        return 0

    lax.fori_loop(1, NV, send_t, 0)

    pltpu.make_async_copy(recv2.at[0 : NZC - 1], recv2.at[0 : NZC - 1], r2).wait()
    c = recv2[...].astype(F32).reshape(64, 128)
    lane = lax.broadcasted_iota(jnp.int32, (64, 128), 1)
    row = lax.broadcasted_iota(jnp.int32, (64, 128), 0)
    c = jnp.where((row == 0) & (lane < 6), 0.5 * c, c)
    lane = lane & 31
    field = (lane - 6 * ((lane * 43) >> 8)) >> 1
    lhs = jnp.concatenate([jnp.where(field == f, c, 0.0) for f in range(3)], axis=0).astype(BF16)
    lhs = jnp.concatenate([lhs, lhs], axis=1)
    z = jnp.dot(lhs, rhs[...], preferred_element_type=F32)
    level_weight = lw[0]
    for f in range(3):
        g = jnp.sum(
            z[64 * f : 64 * f + 64, 0:LON_W] * ebuf[0] - z[64 * f : 64 * f + 64, LON_W:] * ebuf[1],
            axis=0, keepdims=True)
        grid_o[0, f] = g
        if f < 2:
            for j in range(4):
                wrow[4 * f + j : 4 * f + j + 1, :] = level_weight * g[:, 128 * j : 128 * j + 128]

    wsend[...] = wrow[...].astype(BF16)
    for t in plane_partners(x, y):
        pltpu.make_async_remote_copy(
            src_ref=wsend, dst_ref=wrecv.at[xy], send_sem=sw, recv_sem=rw,
            device_id={"band": t * NZC + zc, "lev": v}, device_id_type=MESH).start()
    wrecv[xy] = wsend[...]

    pltpu.make_async_copy(wrecv.at[0 : NXY - 1], wrecv.at[0 : NXY - 1], rw).wait()
    wtab[...] = wrecv[...].astype(F32).reshape(8 * NXY, 128)
    table = jnp.concatenate(
        [
            jnp.concatenate([wtab[pl.ds(4 * f + j, NXY, stride=8), :] for j in range(4)], axis=1)
            for f in range(2)
        ],
        axis=0,
    ).astype(BF16)
    lat = lax.broadcasted_iota(jnp.int32, (NXY, 128), 0) * NZC + zc
    others = [lax.rem(v + d, NV) for d in (2, 1, 3, 0)]
    for i in range(NZC):
        g = lax.rem(zc + i, NZC)
        for h in range(2):
            found = jnp.dot(table, onehot[g * 2 + h], preferred_element_type=F32)
            for j in range(2):
                point = coup_v[g, pl.ds(2 * h + j, 1), :] >> 9
                mine = lat == point
                for f in range(2):
                    picked = jnp.where(mine, found[32 * f : 32 * f + 32, 128 * j : 128 * j + 128], 0.0)
                    line = 4 * f + 2 * h + j
                    rrow[i, line : line + 1, :] = jnp.sum(picked, axis=0, keepdims=True)
        rsend[g] = rrow[i].astype(BF16)
        for vv in others[: 4 if i else 3]:
            pltpu.make_async_remote_copy(
                src_ref=rsend.at[g], dst_ref=rrecv.at[zp], send_sem=sr, recv_sem=rr,
                device_id={"band": xy * NZC + g, "lev": vv}, device_id_type=MESH).start()
    rrecv[zp] = rsend[zc]

    pltpu.make_async_copy(trecv.at[0 : NV - 1], trecv.at[0 : NV - 1], rs).wait()
    total = tsum[...]
    for j in range(1, NV):
        total = total + trecv[lax.rem(v + j, NV)].astype(F32).reshape(HALF, 8, 128)
    tsum[...] = total

    pltpu.make_async_copy(rrecv.at[0 : NZ - 1], rrecv.at[0 : NZ - 1], rr).wait()
    wind = jnp.sum(rrecv[...].astype(F32), axis=0)
    turned = pltpu.roll(wind, 4, 0)
    low8 = lax.broadcasted_iota(jnp.int32, (8, 128), 0) < 4
    east8 = jnp.where(low8, -wind, turned)
    north8 = jnp.where(low8, -turned, wind)
    push = jnp.maximum(trig[0] * east8[None] + trig[1] * north8[None], 0.0)
    stress = jnp.sum(push * tsum[...], axis=0)
    mean = (stress + pltpu.roll(stress, 4, 0)) * land8[0] * (1.0 / (NF * ND))
    charnock = 0.011 + 0.5 * mean / (mean + 0.05 * (1.0 + wind * wind + turned * turned))
    char_o[...] = charnock[0:4]

    def result(f, _):
        s = state[f]
        s = s + s * (rate[f] * push)
        out_o[f, 0:HALF] = s[:, 4:8, :]
        out_o[f, HALF:] = s[:, 0:4, :]
        return 0

    lax.fori_loop(0, NF // NV, result, 0)

    halo_up.wait_send()
    halo_down.wait_send()
    pltpu.make_async_copy(coup_v.at[0:7], coup_v.at[0:7], sc).wait()
    pltpu.make_async_copy(recv1.at[0 : NXY - 1], recv1.at[0 : NXY - 1], s1).wait()
    pltpu.make_async_copy(send2.at[0 : NZC - 1], send2.at[0 : NZC - 1], s2).wait()
    pltpu.make_async_copy(wrecv.at[0 : NXY - 1], wrecv.at[0 : NXY - 1], sw).wait()
    pltpu.make_async_copy(rrecv.at[0 : NZ - 1], rrecv.at[0 : NZ - 1], sr).wait()
    pltpu.make_async_copy(trecv.at[0 : NV - 1], trecv.at[0 : NV - 1], ss).wait()


def write(grid, out, char, grid_o, out_o, char_o, sems):
    pieces = [(out.at[i : i + 3], out_o.at[i : i + 3]) for i in range(0, NF // NV, 3)]
    copies = [
        pltpu.make_async_copy(s, d, sems.at[i])
        for i, (s, d) in enumerate((*pieces, (grid, grid_o), (char, char_o)))
    ]
    for c in copies:
        c.start()
    for c in copies:
        c.wait()


def on_device(spectral, legendre, level_weights, coupling, land_sea, spectra, courant, growth_rate, breaking):
    spec = jnp.transpose(spectral, (0, 2, 3, 1, 4)).reshape(15, 2, N)
    hbm, vm = (pl.BlockSpec(memory_space=s) for s in (pltpu.HBM, pltpu.VMEM))
    sm = pltpu.SMEM
    dma = pltpu.SemaphoreType.DMA
    nf = NF // NV
    shapes = (
        jax.ShapeDtypeStruct((1, 3, 1, LON_W), F32),
        jax.ShapeDtypeStruct((nf, ND, 4, 128), F32),
        jax.ShapeDtypeStruct((4, 128), F32),
    )
    grid, out, char = pl.pallas_call(
        kernel,
        out_shape=shapes,
        in_specs=[pl.BlockSpec(memory_space=sm)] + [hbm] * 8,
        out_specs=(vm, vm, vm),
        scratch_shapes=[
            pltpu.VMEM((5, NLAT, N), BF16),
            pltpu.VMEM((15, 2, N), BF16),
            pltpu.VMEM((NZC, 4, 128), jnp.int32),
            pltpu.VMEM((4, 128), jnp.int32),
            pltpu.VMEM((nf, ND, 4, 128), BF16),
            pltpu.VMEM((32, N), F32),
            pltpu.VMEM((NXY, 8, 128), BF16),
            pltpu.VMEM((NXY, 8, 128), BF16),
            pltpu.VMEM((64, 128), F32),
            pltpu.VMEM((NZC, 8, 128), BF16),
            pltpu.VMEM((NZC, 8, 128), BF16),
            pltpu.VMEM((256, 2 * LON_W), BF16),
            pltpu.VMEM((2, 64, LON_W), F32),
            pltpu.VMEM((8, 128), F32),
            pltpu.VMEM((8, 128), BF16),
            pltpu.VMEM((NXY, 8, 128), BF16),
            pltpu.VMEM((8 * NXY, 128), F32),
            pltpu.VMEM((2 * NZC, LON_W, 256), BF16),
            pltpu.VMEM((NZC, 8, 128), F32),
            pltpu.VMEM((NZC, 8, 128), BF16),
            pltpu.VMEM((NZ, 8, 128), BF16),
            pltpu.VMEM((2, nf, HALF, 4, 128), BF16),
            pltpu.VMEM((2, HALF, 8, 128), F32),
            pltpu.VMEM((2, HALF, 8, 128), F32),
            pltpu.VMEM((nf, HALF, 8, 128), F32),
            pltpu.VMEM((HALF, 8, 128), F32),
            pltpu.VMEM((HALF * 8, 128), BF16),
            pltpu.VMEM((NV, HALF * 8, 128), BF16),
            sm((nf,), F32), sm((nf,), F32), sm((nf,), F32),
            dma((5,)), dma((8,)),
            dma, dma, dma, dma, dma, dma, dma, dma,
            dma((2,)), dma((2,)), dma, dma, dma, dma,
        ],
        compiler_params=pltpu.CompilerParams(
            collective_id=0, has_side_effects=True, vmem_limit_bytes=40 * 1024 * 1024
        ),
    )(
        level_weights,
        *(
            pltpu.with_memory_space_constraint(a, pltpu.HBM)
            for a in (spec, legendre, coupling, land_sea, spectra, courant, growth_rate, breaking)
        ),
    )
    grid, out, char = pl.pallas_call(
        write,
        out_shape=shapes,
        in_specs=[vm] * 3,
        out_specs=[hbm] * 3,
        scratch_shapes=[dma((5,))],
        compiler_params=pltpu.CompilerParams(vmem_limit_bytes=16 * 1024 * 1024),
    )(grid, out, char)
    return jnp.transpose(grid, (0, 2, 1, 3)), out, char


def solution(mesh):
    in_specs = (
        P("band", None, "lev", None, None),
        P("band", None, None),
        P("lev"),
        P("band", None),
        P("band", None),
        P("lev", None, "band", None),
        P("lev"),
        P("lev"),
        P("lev"),
    )
    out_specs = (P("band", "lev", None, None), P("lev", None, "band", None), P("band", None))
    return jax.shard_map(on_device, mesh=mesh, in_specs=in_specs, out_specs=out_specs, check_vma=False)
```

```python
import math

import jax
import jax.numpy as jnp
from jax import lax
from jax.experimental import pallas as pl
from jax.experimental.pallas import tpu as pltpu
from jax.sharding import PartitionSpec as P

N = 1280
NLON = 5136
LON_W = 512
NLAT = 256
NF = 36
ND = 36
STEPS = 4
NX, NY, NZC, NV = 4, 8, 8, 4
NB = NX * NY * NZC
NXY = NX * NY
NZ = NV * NZC
HALF = ND // 2
MESH = pl.DeviceIdType.MESH
F32, BF16 = jnp.float32, jnp.bfloat16


def turn(t):
    u = (t - jnp.floor(t + 0.5)) * (2.0 * math.pi)
    s = u * u
    even = jnp.full_like(u, 1.0 / math.factorial(16))
    odd = jnp.full_like(u, -1.0 / math.factorial(17 - 2))
    for k in range(7, -1, -1):
        even = even * s + (-1.0) ** k / math.factorial(2 * k)
        if k < 7:
            odd = odd * s + (-1.0) ** k / math.factorial(2 * k + 1)
    return even, u * odd


def cycles(product):
    return (product - jnp.floor(product * (1.0 / NLON)) * NLON) * (1.0 / NLON)


def plane_partners(x, y):
    xs = [lax.rem(x + d, NX) * NY for d in (2, 3, 1, 0)]
    for dy in (4, 5, 3, 6, 2, 7, 1, 0):
        yy = lax.rem(y + dy, NY)
        for xx in xs[: 4 if dy else 3]:
            yield xx + yy


def kernel(
    lw, spec, leg, coup, land, spectra, cour_h, rate_h, brk_h,
    grid_o, out_o, char_o,
    leg_v, spec_v, coup_v, land_v, own_v, s32, proj, recv1, pack, send2, recv2,
    rhs, ebuf, wrow, wsend, wrecv, wtab, onehot, rrow, rsend, rrecv, halo, ext, trig, state, tsum, tsend, trecv,
    cour, rate, brk,
    leg_s, in_s, s1, r1, s2, r2, sw, rw, sr, rr, sh, rh, sc, rc, ss, rs, heard, told,
):
    b = lax.axis_index("band")
    v = lax.axis_index("lev")
    xy = b // NZC
    x = xy // NY
    y = lax.rem(xy, NY)
    zc = lax.rem(b, NZC)
    zp = v * NZC + zc
    up = lax.rem(b + 1, NB)
    down = lax.rem(b + NB - 1, NB)

    loads = [pltpu.make_async_copy(leg.at[m], leg_v.at[m], leg_s.at[m]) for m in range(5)]
    spec_c = pltpu.make_async_copy(spec, spec_v, in_s.at[0])
    coup_c = pltpu.make_async_copy(coup, coup_v.at[zc], in_s.at[1])
    land_c = pltpu.make_async_copy(land, land_v, in_s.at[2])
    own_c = pltpu.make_async_copy(spectra, own_v, in_s.at[3])
    scalars = [
        pltpu.make_async_copy(h, t, in_s.at[4 + i])
        for i, (h, t) in enumerate(((cour_h, cour), (rate_h, rate), (brk_h, brk)))
    ]
    barrier = pltpu.get_barrier_semaphore()

    for t in plane_partners(x, y):
        pl.semaphore_signal(barrier, inc=1, device_id={"band": t * NZC + zc, "lev": v}, device_id_type=MESH)
    near = [lax.rem(v + d, NV) for d in (1, NV - 1)]
    for vv in near:
        pl.semaphore_signal(barrier, inc=1, device_id={"band": b, "lev": vv}, device_id_type=MESH)
    mates = [xy * NZC + lax.rem(zc + d, NZC) for d in (4, 3, 5, 2, 6, 1, 7)]
    for t in mates:
        pl.semaphore_signal(barrier, inc=1, device_id={"band": t, "lev": v}, device_id_type=MESH)
    pl.semaphore_signal(barrier, inc=1, device_id={"band": up, "lev": v}, device_id_type=MESH)
    pl.semaphore_signal(barrier, inc=1, device_id={"band": down, "lev": v}, device_id_type=MESH)

    spec_c.start()
    for c in (*loads, coup_c, land_c, own_c, *scalars):
        c.start()

    spec_c.wait()
    s32[30:32, :] = jnp.zeros((2, N), F32)
    for j in range(15):
        s32[2 * j : 2 * j + 2, :] = spec_v[j].astype(F32)
    sl = lax.broadcasted_iota(jnp.int32, (128, N), 0)
    held = s32[...]
    held = jnp.concatenate([held, held, held, held], axis=0)
    sm = ((sl & 31) * 43) >> 8
    held = jnp.where((sl >> 5) == x, held, 0.0)
    acc = None
    for m in range(5):
        s_m = jnp.where(sm == m, held, 0.0).astype(BF16)
        loads[m].wait()
        d = lax.dot_general(leg_v[m], s_m, (((1,), (1,)), ((), ())), preferred_element_type=F32)
        acc = d if acc is None else acc + d
    proj[...] = acc.reshape(NXY, 8, 128).astype(BF16)

    pl.semaphore_wait(barrier, NXY - 1 + 2 + NZC - 1 + 2)

    for t in plane_partners(x, y):
        pltpu.make_async_remote_copy(
            src_ref=proj.at[t], dst_ref=recv1.at[xy], send_sem=s1, recv_sem=r1,
            device_id={"band": t * NZC + zc, "lev": v}, device_id_type=MESH).start()
    recv1[xy] = proj[xy]

    for vv in near:
        pl.semaphore_signal(heard, inc=1, device_id={"band": b, "lev": vv}, device_id_type=MESH)

    halo_up = pltpu.make_async_remote_copy(
        src_ref=spectra.at[:, 0:HALF], dst_ref=halo.at[0], send_sem=sh.at[0], recv_sem=rh.at[0],
        device_id={"band": up, "lev": v}, device_id_type=MESH)
    halo_down = pltpu.make_async_remote_copy(
        src_ref=spectra.at[:, HALF:], dst_ref=halo.at[1], send_sem=sh.at[1], recv_sem=rh.at[1],
        device_id={"band": down, "lev": v}, device_id_type=MESH)

    def send_coup(j, _):
        t = lax.rem(zc + j, NZC)
        pltpu.make_async_remote_copy(
            src_ref=coup, dst_ref=coup_v.at[zc], send_sem=sc, recv_sem=rc,
            device_id={"band": xy * NZC + t, "lev": v}, device_id_type=MESH).start()
        return 0

    lax.fori_loop(1, NZC, send_coup, 0)
    halo_up.start()
    halo_down.start()

    slot = lax.broadcasted_iota(jnp.int32, (128, LON_W), 0)
    lon = lax.broadcasted_iota(jnp.int32, (128, LON_W), 1).astype(F32)
    xs = slot >> 5
    slot = slot & 31
    mi = (slot * 43) >> 8
    k = (xs * 320 + mi).astype(F32)
    part = (slot & 1).astype(F32)
    re, im = turn(cycles(k * lon) + 0.25 * part)
    re_hi, im_hi = re.astype(BF16), im.astype(BF16)
    rhs[0:128, 0:LON_W] = re_hi
    rhs[0:128, LON_W:] = im_hi
    rhs[128:256, 0:LON_W] = (re - re_hi.astype(F32)).astype(BF16)
    rhs[128:256, LON_W:] = (im - im_hi.astype(F32)).astype(BF16)
    q = lax.broadcasted_iota(jnp.int32, (64, LON_W), 0)
    q = ((q & 7) * 8 + (q >> 3)).astype(F32)
    lon = lax.broadcasted_iota(jnp.int32, (64, LON_W), 1).astype(F32)
    ec, es = turn(cycles(q * 5.0 * lon))
    ebuf[0] = 2.0 * ec
    ebuf[1] = 2.0 * es
    e = lax.broadcasted_iota(jnp.int32, (HALF, 8, 128), 0).astype(F32)
    tc, ts = turn((e + 0.5) * (1.0 / ND))
    trig[0] = tc
    trig[1] = ts

    coup_c.wait()
    pltpu.make_async_copy(coup_v.at[0:7], coup_v.at[0:7], rc).wait()
    lon_i = lax.broadcasted_iota(jnp.int32, (LON_W, 128), 0)

    def hot(g, _):
        for j in range(4):
            point = coup_v[g, pl.ds(j, 1), :] & (LON_W - 1)
            onehot[g * 2 + j // 2, :, (j % 2) * 128 : (j % 2) * 128 + 128] = jnp.where(
                lon_i == point, 1.0, 0.0).astype(BF16)
        return 0

    lax.fori_loop(0, NZC, hot, 0)

    pltpu.make_async_copy(recv1.at[0 : NXY - 1], recv1.at[0 : NXY - 1], r1).wait()
    for j in range(NY):
        parts = [recv1[8 * i + j].astype(F32) for i in range(NX)]
        pack[j * 8 : j * 8 + 8, :] = (parts[0] + parts[1]) + (parts[2] + parts[3])
    for j in range(NZC):
        send2[j] = pack[pl.ds(j, NY, stride=NZC), :].astype(BF16)

    for j in (4, 3, 5, 2, 6, 1, 7):
        t = lax.rem(zc + j, NZC)
        pltpu.make_async_remote_copy(
            src_ref=send2.at[t], dst_ref=recv2.at[zc], send_sem=s2, recv_sem=r2,
            device_id={"band": xy * NZC + t, "lev": v}, device_id_type=MESH).start()
    recv2[zc] = send2[zc]

    pl.semaphore_wait(heard, 2)
    for t in mates:
        pl.semaphore_signal(told, inc=1, device_id={"band": t, "lev": v}, device_id_type=MESH)

    land_c.wait()
    own_c.wait()
    for c in scalars:
        c.wait()
    halo_up.wait_recv()
    halo_down.wait_recv()
    low = lax.broadcasted_iota(jnp.int32, (HALF, 8, 128), 1) < 4
    land_f = land_v[...].astype(F32)
    land8 = jnp.concatenate([land_f, land_f], axis=0)[None]
    quarter = HALF // 2
    tsum[...] = jnp.zeros((HALF, 8, 128), F32)
    first = v * (NF // NV)

    def waves(f, _):
        ext[0, :, 0:4, :] = jnp.where(b == 0, 0.0, halo[0, f].astype(F32))
        ext[0, :, 4:8, :] = own_v[f, 0:HALF].astype(F32)
        ext[1, :, 0:4, :] = own_v[f, HALF:].astype(F32)
        ext[1, :, 4:8, :] = jnp.where(b == NB - 1, 0.0, halo[1, f].astype(F32))
        speed = cour[f]
        both = []
        for side in range(2):
            parts = []
            for p in range(2):
                span = slice(p * quarter, (p + 1) * quarter)
                s = ext[side, span]
                a = speed * jnp.abs(trig[0, span])
                c = speed * trig[1, span]
                rest = 1.0 - a - c
                east = 1 if side == p else 127
                north = 1 if side == 0 else 7
                for _ in range(STEPS):
                    s = rest * s + a * pltpu.roll(s, east, 2) + c * pltpu.roll(s, north, 1)
                parts.append(s)
            both.append(jnp.concatenate(parts, axis=0))
        s = jnp.where(low, both[1], both[0])
        energy = 1.0 + 2.0 * (first + f).astype(F32) / (NF - 1)
        tsum[...] += (energy * rate[f]) * s
        state[f] = land8 * s / (1.0 + brk[f] * s)
        return 0

    lax.fori_loop(0, NF // NV, waves, 0)
    tsend[...] = tsum[...].reshape(HALF * 8, 128).astype(BF16)

    def send_t(j, _):
        t = lax.rem(v + j, NV)
        pltpu.make_async_remote_copy(
            src_ref=tsend, dst_ref=trecv.at[v], send_sem=ss, recv_sem=rs,
            device_id={"band": b, "lev": t}, device_id_type=MESH).start()
        return 0

    lax.fori_loop(1, NV, send_t, 0)

    pltpu.make_async_copy(recv2.at[0 : NZC - 1], recv2.at[0 : NZC - 1], r2).wait()
    c = recv2[...].astype(F32).reshape(64, 128)
    lane = lax.broadcasted_iota(jnp.int32, (64, 128), 1)
    row = lax.broadcasted_iota(jnp.int32, (64, 128), 0)
    c = jnp.where((row == 0) & (lane < 6), 0.5 * c, c)
    lane = lane & 31
    field = (lane - 6 * ((lane * 43) >> 8)) >> 1
    level_weight = lw[0]

    def synthesis(fields):
        lhs = jnp.concatenate([jnp.where(field == f, c, 0.0) for f in fields], axis=0).astype(BF16)
        z = jnp.dot(jnp.concatenate([lhs, lhs], axis=1), rhs[...], preferred_element_type=F32)
        return [
            jnp.sum(
                z[64 * i : 64 * i + 64, 0:LON_W] * ebuf[0] - z[64 * i : 64 * i + 64, LON_W:] * ebuf[1],
                axis=0, keepdims=True)
            for i in range(len(fields))
        ]

    winds = synthesis((0, 1))
    for f in range(2):
        for j in range(4):
            wrow[4 * f + j : 4 * f + j + 1, :] = level_weight * winds[f][:, 128 * j : 128 * j + 128]
    wsend[...] = wrow[...].astype(BF16)
    for t in plane_partners(x, y):
        pltpu.make_async_remote_copy(
            src_ref=wsend, dst_ref=wrecv.at[xy], send_sem=sw, recv_sem=rw,
            device_id={"band": t * NZC + zc, "lev": v}, device_id_type=MESH).start()
    wrecv[xy] = wsend[...]
    for f, g in enumerate((*winds, *synthesis((2,)))):
        grid_o[0, f] = g

    pltpu.make_async_copy(wrecv.at[0 : NXY - 1], wrecv.at[0 : NXY - 1], rw).wait()
    wtab[...] = wrecv[...].astype(F32).reshape(8 * NXY, 128)
    table = jnp.concatenate(
        [
            jnp.concatenate([wtab[pl.ds(4 * f + j, NXY, stride=8), :] for j in range(4)], axis=1)
            for f in range(2)
        ],
        axis=0,
    ).astype(BF16)
    lat = lax.broadcasted_iota(jnp.int32, (NXY, 128), 0) * NZC + zc
    pl.semaphore_wait(told, NZC - 1)
    others = [lax.rem(v + d, NV) for d in (2, 1, 3, 0)]
    bands = [lax.rem(zc + i, NZC) for i in range(NZC)]

    def products(g):
        return [jnp.dot(table, onehot[g * 2 + h], preferred_element_type=F32) for h in range(2)]

    ready = products(bands[0])
    for i, g in enumerate(bands):
        found = ready
        if i + 1 < NZC:
            ready = products(bands[i + 1])
        for line in range(4):
            h, j = line // 2, line % 2
            mine = lat == (coup_v[g, pl.ds(line, 1), :] >> 9)
            for f in range(2):
                picked = jnp.where(mine, found[h][32 * f : 32 * f + 32, 128 * j : 128 * j + 128], 0.0)
                rrow[i, 4 * f + line : 4 * f + line + 1, :] = jnp.sum(picked, axis=0, keepdims=True)
        rsend[g] = rrow[i].astype(BF16)
        for vv in others[: 4 if i else 3]:
            pltpu.make_async_remote_copy(
                src_ref=rsend.at[g], dst_ref=rrecv.at[zp], send_sem=sr, recv_sem=rr,
                device_id={"band": xy * NZC + g, "lev": vv}, device_id_type=MESH).start()
    rrecv[zp] = rsend[zc]

    pltpu.make_async_copy(trecv.at[0 : NV - 1], trecv.at[0 : NV - 1], rs).wait()
    total = tsum[...]
    for j in range(1, NV):
        total = total + trecv[lax.rem(v + j, NV)].astype(F32).reshape(HALF, 8, 128)
    tsum[...] = total

    pltpu.make_async_copy(rrecv.at[0 : NZ - 1], rrecv.at[0 : NZ - 1], rr).wait()
    wind = jnp.sum(rrecv[...].astype(F32), axis=0)
    turned = pltpu.roll(wind, 4, 0)
    low8 = lax.broadcasted_iota(jnp.int32, (8, 128), 0) < 4
    east8 = jnp.where(low8, -wind, turned)
    north8 = jnp.where(low8, -turned, wind)
    push = jnp.maximum(trig[0] * east8[None] + trig[1] * north8[None], 0.0)
    stress = jnp.sum(push * tsum[...], axis=0)
    mean = (stress + pltpu.roll(stress, 4, 0)) * land8[0] * (1.0 / (NF * ND))
    charnock = 0.011 + 0.5 * mean / (mean + 0.05 * (1.0 + wind * wind + turned * turned))
    char_o[...] = charnock[0:4]

    def result(f, _):
        s = state[f]
        s = s + s * (rate[f] * push)
        out_o[f, 0:HALF] = s[:, 4:8, :]
        out_o[f, HALF:] = s[:, 0:4, :]
        return 0

    lax.fori_loop(0, NF // NV, result, 0)

    halo_up.wait_send()
    halo_down.wait_send()
    pltpu.make_async_copy(coup_v.at[0:7], coup_v.at[0:7], sc).wait()
    pltpu.make_async_copy(recv1.at[0 : NXY - 1], recv1.at[0 : NXY - 1], s1).wait()
    pltpu.make_async_copy(send2.at[0 : NZC - 1], send2.at[0 : NZC - 1], s2).wait()
    pltpu.make_async_copy(wrecv.at[0 : NXY - 1], wrecv.at[0 : NXY - 1], sw).wait()
    pltpu.make_async_copy(rrecv.at[0 : NZ - 1], rrecv.at[0 : NZ - 1], sr).wait()
    pltpu.make_async_copy(trecv.at[0 : NV - 1], trecv.at[0 : NV - 1], ss).wait()


def write(grid, out, char, grid_o, out_o, char_o, sems):
    pieces = [(out.at[i : i + 3], out_o.at[i : i + 3]) for i in range(0, NF // NV, 3)]
    copies = [
        pltpu.make_async_copy(s, d, sems.at[i])
        for i, (s, d) in enumerate((*pieces, (grid, grid_o), (char, char_o)))
    ]
    for c in copies:
        c.start()
    for c in copies:
        c.wait()


def on_device(spectral, legendre, level_weights, coupling, land_sea, spectra, courant, growth_rate, breaking):
    spec = jnp.transpose(spectral, (0, 2, 3, 1, 4)).reshape(15, 2, N)
    hbm, vm = (pl.BlockSpec(memory_space=s) for s in (pltpu.HBM, pltpu.VMEM))
    sm = pltpu.SMEM
    dma = pltpu.SemaphoreType.DMA
    nf = NF // NV
    shapes = (
        jax.ShapeDtypeStruct((1, 3, 1, LON_W), F32),
        jax.ShapeDtypeStruct((nf, ND, 4, 128), F32),
        jax.ShapeDtypeStruct((4, 128), F32),
    )
    grid, out, char = pl.pallas_call(
        kernel,
        out_shape=shapes,
        in_specs=[pl.BlockSpec(memory_space=sm)] + [hbm] * 8,
        out_specs=(vm, vm, vm),
        scratch_shapes=[
            pltpu.VMEM((5, NLAT, N), BF16),
            pltpu.VMEM((15, 2, N), BF16),
            pltpu.VMEM((NZC, 4, 128), jnp.int32),
            pltpu.VMEM((4, 128), jnp.int32),
            pltpu.VMEM((nf, ND, 4, 128), BF16),
            pltpu.VMEM((32, N), F32),
            pltpu.VMEM((NXY, 8, 128), BF16),
            pltpu.VMEM((NXY, 8, 128), BF16),
            pltpu.VMEM((64, 128), F32),
            pltpu.VMEM((NZC, 8, 128), BF16),
            pltpu.VMEM((NZC, 8, 128), BF16),
            pltpu.VMEM((256, 2 * LON_W), BF16),
            pltpu.VMEM((2, 64, LON_W), F32),
            pltpu.VMEM((8, 128), F32),
            pltpu.VMEM((8, 128), BF16),
            pltpu.VMEM((NXY, 8, 128), BF16),
            pltpu.VMEM((8 * NXY, 128), F32),
            pltpu.VMEM((2 * NZC, LON_W, 256), BF16),
            pltpu.VMEM((NZC, 8, 128), F32),
            pltpu.VMEM((NZC, 8, 128), BF16),
            pltpu.VMEM((NZ, 8, 128), BF16),
            pltpu.VMEM((2, nf, HALF, 4, 128), BF16),
            pltpu.VMEM((2, HALF, 8, 128), F32),
            pltpu.VMEM((2, HALF, 8, 128), F32),
            pltpu.VMEM((nf, HALF, 8, 128), F32),
            pltpu.VMEM((HALF, 8, 128), F32),
            pltpu.VMEM((HALF * 8, 128), BF16),
            pltpu.VMEM((NV, HALF * 8, 128), BF16),
            sm((nf,), F32), sm((nf,), F32), sm((nf,), F32),
            dma((5,)), dma((8,)),
            dma, dma, dma, dma, dma, dma, dma, dma,
            dma((2,)), dma((2,)), dma, dma, dma, dma,
            pltpu.SemaphoreType.REGULAR, pltpu.SemaphoreType.REGULAR,
        ],
        compiler_params=pltpu.CompilerParams(
            collective_id=0, has_side_effects=True, vmem_limit_bytes=40 * 1024 * 1024
        ),
    )(
        level_weights,
        *(
            pltpu.with_memory_space_constraint(a, pltpu.HBM)
            for a in (spec, legendre, coupling, land_sea, spectra, courant, growth_rate, breaking)
        ),
    )
    grid, out, char = pl.pallas_call(
        write,
        out_shape=shapes,
        in_specs=[vm] * 3,
        out_specs=[hbm] * 3,
        scratch_shapes=[dma((5,))],
        compiler_params=pltpu.CompilerParams(vmem_limit_bytes=16 * 1024 * 1024),
    )(grid, out, char)
    return jnp.transpose(grid, (0, 2, 1, 3)), out, char


def solution(mesh):
    in_specs = (
        P("band", None, "lev", None, None),
        P("band", None, None),
        P("lev"),
        P("band", None),
        P("band", None),
        P("lev", None, "band", None),
        P("lev"),
        P("lev"),
        P("lev"),
    )
    out_specs = (P("band", "lev", None, None), P("lev", None, "band", None), P("band", None))
    return jax.shard_map(on_device, mesh=mesh, in_specs=in_specs, out_specs=out_specs, check_vma=False)
```

```python
import math

import jax
import jax.numpy as jnp
from jax import lax
from jax.experimental import pallas as pl
from jax.experimental.pallas import tpu as pltpu
from jax.sharding import PartitionSpec as P

N = 1280
NLON = 5136
LON_W = 512
NLAT = 256
NF = 36
ND = 36
STEPS = 4
NX, NY, NZC, NV = 4, 8, 8, 4
NB = NX * NY * NZC
NXY = NX * NY
NZ = NV * NZC
HALF = ND // 2
MESH = pl.DeviceIdType.MESH
F32, BF16 = jnp.float32, jnp.bfloat16


def turn(t):
    u = (t - jnp.floor(t + 0.5)) * (2.0 * math.pi)
    s = u * u
    even = jnp.full_like(u, 1.0 / math.factorial(16))
    odd = jnp.full_like(u, -1.0 / math.factorial(17 - 2))
    for k in range(7, -1, -1):
        even = even * s + (-1.0) ** k / math.factorial(2 * k)
        if k < 7:
            odd = odd * s + (-1.0) ** k / math.factorial(2 * k + 1)
    return even, u * odd


def cycles(product):
    return (product - jnp.floor(product * (1.0 / NLON)) * NLON) * (1.0 / NLON)


def plane_partners(x, y):
    xs = [lax.rem(x + d, NX) * NY for d in (2, 3, 1, 0)]
    for dy in (4, 5, 3, 6, 2, 7, 1, 0):
        yy = lax.rem(y + dy, NY)
        for xx in xs[: 4 if dy else 3]:
            yield xx + yy, yy


def kernel(
    lw, spec, leg, coup, land, spectra, cour_h, rate_h, brk_h,
    grid_o, out_o, char_o,
    leg_v, spec_v, coup_v, land_v, own_v, s32, send1, recv1, pack, send2, recv2,
    rhs, ebuf, wrow, wsend, wrecv, wtab, onehot, rrow, rsend, rrecv, halo, ext, trig, state, tsum, tsend, trecv,
    cour, rate, brk,
    leg_s, in_s, s1, r1, s2, r2, sw, rw, sr, rr, sh, rh, sc, rc, ss, rs, heard, told, met, column, whole,
):
    b = lax.axis_index("band")
    v = lax.axis_index("lev")
    xy = b // NZC
    x = xy // NY
    y = lax.rem(xy, NY)
    zc = lax.rem(b, NZC)
    zp = v * NZC + zc
    up = lax.rem(b + 1, NB)
    down = lax.rem(b + NB - 1, NB)

    loads = [pltpu.make_async_copy(leg.at[m], leg_v.at[m], leg_s.at[m]) for m in range(5)]
    spec_c = pltpu.make_async_copy(spec, spec_v, in_s.at[0])
    coup_c = pltpu.make_async_copy(coup, coup_v.at[zc], in_s.at[1])
    land_c = pltpu.make_async_copy(land, land_v, in_s.at[2])
    own_c = pltpu.make_async_copy(spectra, own_v, in_s.at[3])
    scalars = [
        pltpu.make_async_copy(h, t, in_s.at[4 + i])
        for i, (h, t) in enumerate(((cour_h, cour), (rate_h, rate), (brk_h, brk)))
    ]
    barrier = pltpu.get_barrier_semaphore()

    pl.semaphore_signal(barrier, inc=1, device_id={"band": up, "lev": v}, device_id_type=MESH)
    pl.semaphore_signal(barrier, inc=1, device_id={"band": down, "lev": v}, device_id_type=MESH)

    def beside(dx, dy):
        return (lax.rem(x + dx, NX) * NY + lax.rem(y + dy, NY)) * NZC + zc

    sides = [beside(0, 1), beside(0, NY - 1), beside(1, 0), beside(NX - 1, 0)]
    for t in sides:
        pl.semaphore_signal(barrier, inc=1, device_id={"band": t, "lev": v}, device_id_type=MESH)
    near = [lax.rem(v + d, NV) for d in (1, NV - 1)]
    for vv in near:
        pl.semaphore_signal(barrier, inc=1, device_id={"band": b, "lev": vv}, device_id_type=MESH)
    mates = [xy * NZC + lax.rem(zc + d, NZC) for d in (4, 3, 5, 2, 6, 1, 7)]
    for t in mates:
        pl.semaphore_signal(barrier, inc=1, device_id={"band": t, "lev": v}, device_id_type=MESH)

    spec_c.start()
    for c in (*loads, coup_c, land_c, own_c, *scalars):
        c.start()

    spec_c.wait()
    s32[30:32, :] = jnp.zeros((2, N), F32)
    for j in range(15):
        s32[2 * j : 2 * j + 2, :] = spec_v[j].astype(F32)
    sl = lax.broadcasted_iota(jnp.int32, (128, N), 0)
    held = s32[...]
    held = jnp.concatenate([held, held, held, held], axis=0)
    sm = ((sl & 31) * 43) >> 8
    acc = None
    for m in range(5):
        s_m = jnp.where(sm == m, held, 0.0).astype(BF16)
        loads[m].wait()
        d = lax.dot_general(leg_v[m], s_m, (((1,), (1,)), ((), ())), preferred_element_type=F32)
        acc = d if acc is None else acc + d
    group = lax.broadcasted_iota(jnp.int32, (64, 128), 1) >> 5
    packed = acc[0:64]
    for i in range(1, NX):
        packed = jnp.where(group == i, acc[64 * i : 64 * i + 64], packed)
    pack[...] = packed
    for j in range(NZC):
        send1[j] = pack[pl.ds(j, NY, stride=NZC), :].astype(BF16)

    pl.semaphore_wait(barrier, 4 + 2 + NZC - 1 + 2)

    for d in (4, 3, 5, 2, 6, 1, 7):
        t = lax.rem(zc + d, NZC)
        pltpu.make_async_remote_copy(
            src_ref=send1.at[t], dst_ref=recv1.at[zc], send_sem=s1, recv_sem=r1,
            device_id={"band": xy * NZC + t, "lev": v}, device_id_type=MESH).start()
    recv1[zc] = send1[zc]

    for t in sides:
        pl.semaphore_signal(met, inc=1, device_id={"band": t, "lev": v}, device_id_type=MESH)
    for vv in near:
        pl.semaphore_signal(heard, inc=1, device_id={"band": b, "lev": vv}, device_id_type=MESH)

    halo_up = pltpu.make_async_remote_copy(
        src_ref=spectra.at[:, 0:HALF], dst_ref=halo.at[0], send_sem=sh.at[0], recv_sem=rh.at[0],
        device_id={"band": up, "lev": v}, device_id_type=MESH)
    halo_down = pltpu.make_async_remote_copy(
        src_ref=spectra.at[:, HALF:], dst_ref=halo.at[1], send_sem=sh.at[1], recv_sem=rh.at[1],
        device_id={"band": down, "lev": v}, device_id_type=MESH)

    def send_coup(j, _):
        t = lax.rem(zc + j, NZC)
        pltpu.make_async_remote_copy(
            src_ref=coup, dst_ref=coup_v.at[zc], send_sem=sc, recv_sem=rc,
            device_id={"band": xy * NZC + t, "lev": v}, device_id_type=MESH).start()
        return 0

    lax.fori_loop(1, NZC, send_coup, 0)
    halo_up.start()
    halo_down.start()

    slot = lax.broadcasted_iota(jnp.int32, (128, LON_W), 0)
    lon = lax.broadcasted_iota(jnp.int32, (128, LON_W), 1).astype(F32)
    xs = slot >> 5
    slot = slot & 31
    mi = (slot * 43) >> 8
    k = (xs * 320 + mi).astype(F32)
    part = (slot & 1).astype(F32)
    re, im = turn(cycles(k * lon) + 0.25 * part)
    re_hi, im_hi = re.astype(BF16), im.astype(BF16)
    rhs[0:128, 0:LON_W] = re_hi
    rhs[0:128, LON_W:] = im_hi
    rhs[128:256, 0:LON_W] = (re - re_hi.astype(F32)).astype(BF16)
    rhs[128:256, LON_W:] = (im - im_hi.astype(F32)).astype(BF16)
    q = lax.broadcasted_iota(jnp.int32, (64, LON_W), 0).astype(F32)
    lon = lax.broadcasted_iota(jnp.int32, (64, LON_W), 1).astype(F32)
    ec, es = turn(cycles(q * 5.0 * lon))
    ebuf[0] = 2.0 * ec
    ebuf[1] = 2.0 * es
    e = lax.broadcasted_iota(jnp.int32, (HALF, 8, 128), 0).astype(F32)
    tc, ts = turn((e + 0.5) * (1.0 / ND))
    trig[0] = tc
    trig[1] = ts

    pl.semaphore_wait(met, 4)
    for t in (beside(0, 2), beside(0, NY - 2)):
        pl.semaphore_signal(column, inc=1, device_id={"band": t, "lev": v}, device_id_type=MESH)
    pl.semaphore_wait(column, 2)
    for d in range(1, NX):
        pl.semaphore_signal(whole, inc=1, device_id={"band": beside(d, 0), "lev": v}, device_id_type=MESH)

    coup_c.wait()
    pltpu.make_async_copy(coup_v.at[0:7], coup_v.at[0:7], rc).wait()
    lon_i = lax.broadcasted_iota(jnp.int32, (LON_W, 128), 0)

    def hot(g, _):
        for j in range(4):
            point = coup_v[g, pl.ds(j, 1), :] & (LON_W - 1)
            onehot[g * 2 + j // 2, :, (j % 2) * 128 : (j % 2) * 128 + 128] = jnp.where(
                lon_i == point, 1.0, 0.0).astype(BF16)
        return 0

    lax.fori_loop(0, NZC, hot, 0)

    pltpu.make_async_copy(recv1.at[0 : NZC - 1], recv1.at[0 : NZC - 1], r1).wait()
    pack[...] = recv1[...].astype(F32).reshape(64, 128)
    for j in range(NY):
        send2[j] = pack[pl.ds(j, NZC, stride=NY), :].astype(BF16)
    pl.semaphore_wait(whole, NX - 1)
    for t, yy in plane_partners(x, y):
        pltpu.make_async_remote_copy(
            src_ref=send2.at[yy], dst_ref=recv2.at[xy], send_sem=s2, recv_sem=r2,
            device_id={"band": t * NZC + zc, "lev": v}, device_id_type=MESH).start()
    recv2[xy] = send2[y]

    pl.semaphore_wait(heard, 2)
    for t in mates:
        pl.semaphore_signal(told, inc=1, device_id={"band": t, "lev": v}, device_id_type=MESH)

    land_c.wait()
    own_c.wait()
    for c in scalars:
        c.wait()
    halo_up.wait_recv()
    halo_down.wait_recv()
    low = lax.broadcasted_iota(jnp.int32, (HALF, 8, 128), 1) < 4
    land_f = land_v[...].astype(F32)
    land8 = jnp.concatenate([land_f, land_f], axis=0)[None]
    quarter = HALF // 2
    tsum[...] = jnp.zeros((HALF, 8, 128), F32)
    first = v * (NF // NV)

    def waves(f, _):
        ext[0, :, 0:4, :] = jnp.where(b == 0, 0.0, halo[0, f].astype(F32))
        ext[0, :, 4:8, :] = own_v[f, 0:HALF].astype(F32)
        ext[1, :, 0:4, :] = own_v[f, HALF:].astype(F32)
        ext[1, :, 4:8, :] = jnp.where(b == NB - 1, 0.0, halo[1, f].astype(F32))
        speed = cour[f]
        both = []
        for side in range(2):
            parts = []
            for p in range(2):
                span = slice(p * quarter, (p + 1) * quarter)
                s = ext[side, span]
                a = speed * jnp.abs(trig[0, span])
                c = speed * trig[1, span]
                rest = 1.0 - a - c
                east = 1 if side == p else 127
                north = 1 if side == 0 else 7
                for _ in range(STEPS):
                    s = rest * s + a * pltpu.roll(s, east, 2) + c * pltpu.roll(s, north, 1)
                parts.append(s)
            both.append(jnp.concatenate(parts, axis=0))
        s = jnp.where(low, both[1], both[0])
        energy = 1.0 + 2.0 * (first + f).astype(F32) / (NF - 1)
        tsum[...] += (energy * rate[f]) * s
        state[f] = land8 * s / (1.0 + brk[f] * s)
        return 0

    lax.fori_loop(0, NF // NV, waves, 0)
    tsend[...] = tsum[...].reshape(HALF * 8, 128).astype(BF16)

    def send_t(j, _):
        t = lax.rem(v + j, NV)
        pltpu.make_async_remote_copy(
            src_ref=tsend, dst_ref=trecv.at[v], send_sem=ss, recv_sem=rs,
            device_id={"band": b, "lev": t}, device_id_type=MESH).start()
        return 0

    lax.fori_loop(1, NV, send_t, 0)

    pltpu.make_async_copy(recv2.at[0 : NXY - 1], recv2.at[0 : NXY - 1], r2).wait()
    c = jnp.zeros((64, 128), F32)
    for i in range(NX):
        part = recv2[NY * i : NY * i + NY].astype(F32).reshape(64, 128)
        c = jnp.where(group == i, pltpu.roll(part, lax.rem(i - x + NX, NX) * 32, 1), c)
    lane = lax.broadcasted_iota(jnp.int32, (64, 128), 1)
    row = lax.broadcasted_iota(jnp.int32, (64, 128), 0)
    c = jnp.where((row == 0) & (lane < 6), 0.5 * c, c)
    lane = lane & 31
    field = (lane - 6 * ((lane * 43) >> 8)) >> 1
    level_weight = lw[0]

    def synthesis(fields):
        lhs = jnp.concatenate([jnp.where(field == f, c, 0.0) for f in fields], axis=0).astype(BF16)
        z = jnp.dot(jnp.concatenate([lhs, lhs], axis=1), rhs[...], preferred_element_type=F32)
        return [
            jnp.sum(
                z[64 * i : 64 * i + 64, 0:LON_W] * ebuf[0] - z[64 * i : 64 * i + 64, LON_W:] * ebuf[1],
                axis=0, keepdims=True)
            for i in range(len(fields))
        ]

    winds = synthesis((0, 1))
    for f in range(2):
        for j in range(4):
            wrow[4 * f + j : 4 * f + j + 1, :] = level_weight * winds[f][:, 128 * j : 128 * j + 128]
    wsend[...] = wrow[...].astype(BF16)
    for t, _ in plane_partners(x, y):
        pltpu.make_async_remote_copy(
            src_ref=wsend, dst_ref=wrecv.at[xy], send_sem=sw, recv_sem=rw,
            device_id={"band": t * NZC + zc, "lev": v}, device_id_type=MESH).start()
    wrecv[xy] = wsend[...]
    for f, g in enumerate((*winds, *synthesis((2,)))):
        grid_o[0, f] = g

    pltpu.make_async_copy(wrecv.at[0 : NXY - 1], wrecv.at[0 : NXY - 1], rw).wait()
    wtab[...] = wrecv[...].astype(F32).reshape(8 * NXY, 128)
    table = jnp.concatenate(
        [
            jnp.concatenate([wtab[pl.ds(4 * f + j, NXY, stride=8), :] for j in range(4)], axis=1)
            for f in range(2)
        ],
        axis=0,
    ).astype(BF16)
    lat = lax.broadcasted_iota(jnp.int32, (NXY, 128), 0) * NZC + zc
    pl.semaphore_wait(told, NZC - 1)
    others = [lax.rem(v + d, NV) for d in (2, 1, 3, 0)]
    bands = [lax.rem(zc + i, NZC) for i in range(NZC)]

    def products(g):
        return [jnp.dot(table, onehot[g * 2 + h], preferred_element_type=F32) for h in range(2)]

    ready = products(bands[0])
    for i, g in enumerate(bands):
        found = ready
        if i + 1 < NZC:
            ready = products(bands[i + 1])
        for line in range(4):
            h, j = line // 2, line % 2
            mine = lat == (coup_v[g, pl.ds(line, 1), :] >> 9)
            for f in range(2):
                picked = jnp.where(mine, found[h][32 * f : 32 * f + 32, 128 * j : 128 * j + 128], 0.0)
                rrow[i, 4 * f + line : 4 * f + line + 1, :] = jnp.sum(picked, axis=0, keepdims=True)
        rsend[g] = rrow[i].astype(BF16)
        for vv in others[: 4 if i else 3]:
            pltpu.make_async_remote_copy(
                src_ref=rsend.at[g], dst_ref=rrecv.at[zp], send_sem=sr, recv_sem=rr,
                device_id={"band": xy * NZC + g, "lev": vv}, device_id_type=MESH).start()
    rrecv[zp] = rsend[zc]

    pltpu.make_async_copy(trecv.at[0 : NV - 1], trecv.at[0 : NV - 1], rs).wait()
    total = tsum[...]
    for j in range(1, NV):
        total = total + trecv[lax.rem(v + j, NV)].astype(F32).reshape(HALF, 8, 128)
    tsum[...] = total

    pltpu.make_async_copy(rrecv.at[0 : NZ - 1], rrecv.at[0 : NZ - 1], rr).wait()
    wind = jnp.sum(rrecv[...].astype(F32), axis=0)
    turned = pltpu.roll(wind, 4, 0)
    low8 = lax.broadcasted_iota(jnp.int32, (8, 128), 0) < 4
    east8 = jnp.where(low8, -wind, turned)
    north8 = jnp.where(low8, -turned, wind)
    push = jnp.maximum(trig[0] * east8[None] + trig[1] * north8[None], 0.0)
    stress = jnp.sum(push * tsum[...], axis=0)
    mean = (stress + pltpu.roll(stress, 4, 0)) * land8[0] * (1.0 / (NF * ND))
    charnock = 0.011 + 0.5 * mean / (mean + 0.05 * (1.0 + wind * wind + turned * turned))
    char_o[...] = charnock[0:4]

    def result(f, _):
        s = state[f]
        s = s + s * (rate[f] * push)
        out_o[f, 0:HALF] = s[:, 4:8, :]
        out_o[f, HALF:] = s[:, 0:4, :]
        return 0

    lax.fori_loop(0, NF // NV, result, 0)

    halo_up.wait_send()
    halo_down.wait_send()
    pltpu.make_async_copy(coup_v.at[0:7], coup_v.at[0:7], sc).wait()
    pltpu.make_async_copy(recv1.at[0 : NZC - 1], recv1.at[0 : NZC - 1], s1).wait()
    pltpu.make_async_copy(recv2.at[0 : NXY - 1], recv2.at[0 : NXY - 1], s2).wait()
    pltpu.make_async_copy(wrecv.at[0 : NXY - 1], wrecv.at[0 : NXY - 1], sw).wait()
    pltpu.make_async_copy(rrecv.at[0 : NZ - 1], rrecv.at[0 : NZ - 1], sr).wait()
    pltpu.make_async_copy(trecv.at[0 : NV - 1], trecv.at[0 : NV - 1], ss).wait()


def write(grid, out, char, grid_o, out_o, char_o, sems):
    pieces = [(out.at[i : i + 3], out_o.at[i : i + 3]) for i in range(0, NF // NV, 3)]
    copies = [
        pltpu.make_async_copy(s, d, sems.at[i])
        for i, (s, d) in enumerate((*pieces, (grid, grid_o), (char, char_o)))
    ]
    for c in copies:
        c.start()
    for c in copies:
        c.wait()


def on_device(spectral, legendre, level_weights, coupling, land_sea, spectra, courant, growth_rate, breaking):
    spec = jnp.transpose(spectral, (0, 2, 3, 1, 4)).reshape(15, 2, N)
    hbm, vm = (pl.BlockSpec(memory_space=s) for s in (pltpu.HBM, pltpu.VMEM))
    sm = pltpu.SMEM
    dma = pltpu.SemaphoreType.DMA
    nf = NF // NV
    shapes = (
        jax.ShapeDtypeStruct((1, 3, 1, LON_W), F32),
        jax.ShapeDtypeStruct((nf, ND, 4, 128), F32),
        jax.ShapeDtypeStruct((4, 128), F32),
    )
    grid, out, char = pl.pallas_call(
        kernel,
        out_shape=shapes,
        in_specs=[pl.BlockSpec(memory_space=sm)] + [hbm] * 8,
        out_specs=(vm, vm, vm),
        scratch_shapes=[
            pltpu.VMEM((5, NLAT, N), BF16),
            pltpu.VMEM((15, 2, N), BF16),
            pltpu.VMEM((NZC, 4, 128), jnp.int32),
            pltpu.VMEM((4, 128), jnp.int32),
            pltpu.VMEM((nf, ND, 4, 128), BF16),
            pltpu.VMEM((32, N), F32),
            pltpu.VMEM((NZC, 8, 128), BF16),
            pltpu.VMEM((NZC, 8, 128), BF16),
            pltpu.VMEM((64, 128), F32),
            pltpu.VMEM((NY, 8, 128), BF16),
            pltpu.VMEM((NXY, 8, 128), BF16),
            pltpu.VMEM((256, 2 * LON_W), BF16),
            pltpu.VMEM((2, 64, LON_W), F32),
            pltpu.VMEM((8, 128), F32),
            pltpu.VMEM((8, 128), BF16),
            pltpu.VMEM((NXY, 8, 128), BF16),
            pltpu.VMEM((8 * NXY, 128), F32),
            pltpu.VMEM((2 * NZC, LON_W, 256), BF16),
            pltpu.VMEM((NZC, 8, 128), F32),
            pltpu.VMEM((NZC, 8, 128), BF16),
            pltpu.VMEM((NZ, 8, 128), BF16),
            pltpu.VMEM((2, nf, HALF, 4, 128), BF16),
            pltpu.VMEM((2, HALF, 8, 128), F32),
            pltpu.VMEM((2, HALF, 8, 128), F32),
            pltpu.VMEM((nf, HALF, 8, 128), F32),
            pltpu.VMEM((HALF, 8, 128), F32),
            pltpu.VMEM((HALF * 8, 128), BF16),
            pltpu.VMEM((NV, HALF * 8, 128), BF16),
            sm((nf,), F32), sm((nf,), F32), sm((nf,), F32),
            dma((5,)), dma((8,)),
            dma, dma, dma, dma, dma, dma, dma, dma,
            dma((2,)), dma((2,)), dma, dma, dma, dma,
            *[pltpu.SemaphoreType.REGULAR] * 5,
        ],
        compiler_params=pltpu.CompilerParams(
            collective_id=0, has_side_effects=True, vmem_limit_bytes=40 * 1024 * 1024
        ),
    )(
        level_weights,
        *(
            pltpu.with_memory_space_constraint(a, pltpu.HBM)
            for a in (spec, legendre, coupling, land_sea, spectra, courant, growth_rate, breaking)
        ),
    )
    grid, out, char = pl.pallas_call(
        write,
        out_shape=shapes,
        in_specs=[vm] * 3,
        out_specs=[hbm] * 3,
        scratch_shapes=[dma((5,))],
        compiler_params=pltpu.CompilerParams(vmem_limit_bytes=16 * 1024 * 1024),
    )(grid, out, char)
    return jnp.transpose(grid, (0, 2, 1, 3)), out, char


def solution(mesh):
    in_specs = (
        P("band", None, "lev", None, None),
        P("band", None, None),
        P("lev"),
        P("band", None),
        P("band", None),
        P("lev", None, "band", None),
        P("lev"),
        P("lev"),
        P("lev"),
    )
    out_specs = (P("band", "lev", None, None), P("lev", None, "band", None), P("band", None))
    return jax.shard_map(on_device, mesh=mesh, in_specs=in_specs, out_specs=out_specs, check_vma=False)
```

```python
import math

import jax
import jax.numpy as jnp
from jax import lax
from jax.experimental import pallas as pl
from jax.experimental.pallas import tpu as pltpu
from jax.sharding import PartitionSpec as P

N = 1280
NLON = 5136
LON_W = 512
NLAT = 256
NF = 36
ND = 36
STEPS = 4
NX, NY, NZC, NV = 4, 8, 8, 4
NB = NX * NY * NZC
NXY = NX * NY
NZ = NV * NZC
HALF = ND // 2
MESH = pl.DeviceIdType.MESH
F32, BF16 = jnp.float32, jnp.bfloat16


def turn(t):
    u = (t - jnp.floor(t + 0.5)) * (2.0 * math.pi)
    s = u * u
    even = jnp.full_like(u, 1.0 / math.factorial(16))
    odd = jnp.full_like(u, -1.0 / math.factorial(17 - 2))
    for k in range(7, -1, -1):
        even = even * s + (-1.0) ** k / math.factorial(2 * k)
        if k < 7:
            odd = odd * s + (-1.0) ** k / math.factorial(2 * k + 1)
    return even, u * odd


def cycles(product):
    return (product - jnp.floor(product * (1.0 / NLON)) * NLON) * (1.0 / NLON)


def plane_partners(x, y):
    xs = [lax.rem(x + d, NX) * NY for d in (2, 3, 1, 0)]
    for dy in (4, 5, 3, 6, 2, 7, 1, 0):
        yy = lax.rem(y + dy, NY)
        for xx in xs[: 4 if dy else 3]:
            yield xx + yy, yy


def kernel(
    lw, spec, leg, coup, land, spectra, cour_h, rate_h, brk_h,
    grid_o, out_o, char_o,
    leg_v, spec_v, coup_v, land_v, own_v, s32, send1, recv1, pack, send2, recv2,
    rhs, ebuf, wrow, wsend, wrecv, wtab, onehot, rrow, rsend, rrecv, halo, ext, trig, state, tsum, tsend, trecv,
    cour, rate, brk,
    leg_s, in_s, s1, r1, s2, r2, sw, rw, sr, rr, sh, rh, sc, rc, ss, rs, heard, told, met, column, whole,
):
    b = lax.axis_index("band")
    v = lax.axis_index("lev")
    xy = b // NZC
    x = xy // NY
    y = lax.rem(xy, NY)
    zc = lax.rem(b, NZC)
    zp = v * NZC + zc
    up = lax.rem(b + 1, NB)
    down = lax.rem(b + NB - 1, NB)

    loads = [pltpu.make_async_copy(leg.at[m], leg_v.at[m], leg_s.at[m]) for m in range(5)]
    spec_c = pltpu.make_async_copy(spec, spec_v, in_s.at[0])
    coup_c = pltpu.make_async_copy(coup, coup_v.at[zc], in_s.at[1])
    land_c = pltpu.make_async_copy(land, land_v, in_s.at[2])
    own_c = pltpu.make_async_copy(spectra, own_v, in_s.at[3])
    scalars = [
        pltpu.make_async_copy(h, t, in_s.at[4 + i])
        for i, (h, t) in enumerate(((cour_h, cour), (rate_h, rate), (brk_h, brk)))
    ]
    barrier = pltpu.get_barrier_semaphore()

    pl.semaphore_signal(barrier, inc=1, device_id={"band": up, "lev": v}, device_id_type=MESH)
    pl.semaphore_signal(barrier, inc=1, device_id={"band": down, "lev": v}, device_id_type=MESH)

    def beside(dx, dy):
        return (lax.rem(x + dx, NX) * NY + lax.rem(y + dy, NY)) * NZC + zc

    sides = [beside(0, 1), beside(0, NY - 1), beside(1, 0), beside(NX - 1, 0)]
    for t in sides:
        pl.semaphore_signal(barrier, inc=1, device_id={"band": t, "lev": v}, device_id_type=MESH)
    near = [lax.rem(v + d, NV) for d in (1, NV - 1)]
    for vv in near:
        pl.semaphore_signal(barrier, inc=1, device_id={"band": b, "lev": vv}, device_id_type=MESH)
    mates = [xy * NZC + lax.rem(zc + d, NZC) for d in (4, 3, 5, 2, 6, 1, 7)]
    for t in mates:
        pl.semaphore_signal(barrier, inc=1, device_id={"band": t, "lev": v}, device_id_type=MESH)

    spec_c.start()
    for c in (*loads, coup_c, land_c, own_c, *scalars):
        c.start()

    spec_c.wait()
    s32[30:32, :] = jnp.zeros((2, N), F32)
    for j in range(15):
        s32[2 * j : 2 * j + 2, :] = spec_v[j].astype(F32)
    held = s32[...]
    sm = (lax.broadcasted_iota(jnp.int32, (32, N), 0) * 43) >> 8
    acc = None
    for m in range(5):
        s_m = jnp.where(sm == m, held, 0.0).astype(BF16)
        loads[m].wait()
        d = lax.dot_general(leg_v[m], s_m, (((1,), (1,)), ((), ())), preferred_element_type=F32)
        acc = d if acc is None else acc + d
    group = lax.broadcasted_iota(jnp.int32, (64, 128), 1) >> 5
    pack[...] = jnp.concatenate([acc[64 * i : 64 * i + 64] for i in range(NX)], axis=1)
    for j in range(NZC):
        send1[j] = pack[pl.ds(j, NY, stride=NZC), :].astype(BF16)

    pl.semaphore_wait(barrier, 4 + 2 + NZC - 1 + 2)

    for d in (4, 3, 5, 2, 6, 1, 7):
        t = lax.rem(zc + d, NZC)
        pltpu.make_async_remote_copy(
            src_ref=send1.at[t], dst_ref=recv1.at[zc], send_sem=s1, recv_sem=r1,
            device_id={"band": xy * NZC + t, "lev": v}, device_id_type=MESH).start()
    recv1[zc] = send1[zc]

    for t in sides:
        pl.semaphore_signal(met, inc=1, device_id={"band": t, "lev": v}, device_id_type=MESH)
    for vv in near:
        pl.semaphore_signal(heard, inc=1, device_id={"band": b, "lev": vv}, device_id_type=MESH)

    halo_up = pltpu.make_async_remote_copy(
        src_ref=spectra.at[:, 0:HALF], dst_ref=halo.at[0], send_sem=sh.at[0], recv_sem=rh.at[0],
        device_id={"band": up, "lev": v}, device_id_type=MESH)
    halo_down = pltpu.make_async_remote_copy(
        src_ref=spectra.at[:, HALF:], dst_ref=halo.at[1], send_sem=sh.at[1], recv_sem=rh.at[1],
        device_id={"band": down, "lev": v}, device_id_type=MESH)

    def send_coup(j, _):
        t = lax.rem(zc + j, NZC)
        pltpu.make_async_remote_copy(
            src_ref=coup, dst_ref=coup_v.at[zc], send_sem=sc, recv_sem=rc,
            device_id={"band": xy * NZC + t, "lev": v}, device_id_type=MESH).start()
        return 0

    lax.fori_loop(1, NZC, send_coup, 0)
    halo_up.start()
    halo_down.start()

    slot = lax.broadcasted_iota(jnp.int32, (128, LON_W), 0)
    lon = lax.broadcasted_iota(jnp.int32, (128, LON_W), 1).astype(F32)
    xs = slot >> 5
    slot = slot & 31
    mi = (slot * 43) >> 8
    k = (xs * 320 + mi).astype(F32)
    part = (slot & 1).astype(F32)
    re, im = turn(cycles(k * lon) + 0.25 * part)
    re_hi, im_hi = re.astype(BF16), im.astype(BF16)
    rhs[0:128, 0:LON_W] = re_hi
    rhs[0:128, LON_W:] = im_hi
    rhs[128:256, 0:LON_W] = (re - re_hi.astype(F32)).astype(BF16)
    rhs[128:256, LON_W:] = (im - im_hi.astype(F32)).astype(BF16)
    q = lax.broadcasted_iota(jnp.int32, (64, LON_W), 0).astype(F32)
    lon = lax.broadcasted_iota(jnp.int32, (64, LON_W), 1).astype(F32)
    ec, es = turn(cycles(q * 5.0 * lon))
    ebuf[0] = 2.0 * ec
    ebuf[1] = 2.0 * es
    e = lax.broadcasted_iota(jnp.int32, (HALF, 8, 128), 0).astype(F32)
    tc, ts = turn((e + 0.5) * (1.0 / ND))
    trig[0] = tc
    trig[1] = ts

    pl.semaphore_wait(met, 4)
    for t in (beside(0, 2), beside(0, NY - 2)):
        pl.semaphore_signal(column, inc=1, device_id={"band": t, "lev": v}, device_id_type=MESH)
    pl.semaphore_wait(column, 2)
    for d in range(1, NX):
        pl.semaphore_signal(whole, inc=1, device_id={"band": beside(d, 0), "lev": v}, device_id_type=MESH)

    coup_c.wait()
    pltpu.make_async_copy(coup_v.at[0:7], coup_v.at[0:7], rc).wait()
    lon_i = lax.broadcasted_iota(jnp.int32, (LON_W, 128), 0)

    def hot(g, _):
        for j in range(4):
            point = coup_v[g, pl.ds(j, 1), :] & (LON_W - 1)
            onehot[g * 2 + j // 2, :, (j % 2) * 128 : (j % 2) * 128 + 128] = jnp.where(
                lon_i == point, 1.0, 0.0).astype(BF16)
        return 0

    lax.fori_loop(0, NZC, hot, 0)

    pltpu.make_async_copy(recv1.at[0 : NZC - 1], recv1.at[0 : NZC - 1], r1).wait()
    pack[...] = recv1[...].astype(F32).reshape(64, 128)
    for j in range(NY):
        send2[j] = pack[pl.ds(j, NZC, stride=NY), :].astype(BF16)
    pl.semaphore_wait(whole, NX - 1)
    for t, yy in plane_partners(x, y):
        pltpu.make_async_remote_copy(
            src_ref=send2.at[yy], dst_ref=recv2.at[xy], send_sem=s2, recv_sem=r2,
            device_id={"band": t * NZC + zc, "lev": v}, device_id_type=MESH).start()
    recv2[xy] = send2[y]

    pl.semaphore_wait(heard, 2)
    for t in mates:
        pl.semaphore_signal(told, inc=1, device_id={"band": t, "lev": v}, device_id_type=MESH)

    land_c.wait()
    own_c.wait()
    for c in scalars:
        c.wait()
    halo_up.wait_recv()
    halo_down.wait_recv()
    low = lax.broadcasted_iota(jnp.int32, (HALF, 8, 128), 1) < 4
    land_f = land_v[...].astype(F32)
    land8 = jnp.concatenate([land_f, land_f], axis=0)[None]
    quarter = HALF // 2
    tsum[...] = jnp.zeros((HALF, 8, 128), F32)
    first = v * (NF // NV)

    def waves(f, _):
        ext[0, :, 0:4, :] = jnp.where(b == 0, 0.0, halo[0, f].astype(F32))
        ext[0, :, 4:8, :] = own_v[f, 0:HALF].astype(F32)
        ext[1, :, 0:4, :] = own_v[f, HALF:].astype(F32)
        ext[1, :, 4:8, :] = jnp.where(b == NB - 1, 0.0, halo[1, f].astype(F32))
        speed = cour[f]
        both = []
        for side in range(2):
            parts = []
            for p in range(2):
                span = slice(p * quarter, (p + 1) * quarter)
                s = ext[side, span]
                a = speed * jnp.abs(trig[0, span])
                c = speed * trig[1, span]
                rest = 1.0 - a - c
                east = 1 if side == p else 127
                north = 1 if side == 0 else 7
                for _ in range(STEPS):
                    s = rest * s + a * pltpu.roll(s, east, 2) + c * pltpu.roll(s, north, 1)
                parts.append(s)
            both.append(jnp.concatenate(parts, axis=0))
        s = jnp.where(low, both[1], both[0])
        energy = 1.0 + 2.0 * (first + f).astype(F32) / (NF - 1)
        tsum[...] += (energy * rate[f]) * s
        state[f] = land8 * s / (1.0 + brk[f] * s)
        return 0

    lax.fori_loop(0, NF // NV, waves, 0)
    tsend[...] = tsum[...].reshape(HALF * 8, 128).astype(BF16)

    def send_t(j, _):
        t = lax.rem(v + j, NV)
        pltpu.make_async_remote_copy(
            src_ref=tsend, dst_ref=trecv.at[v], send_sem=ss, recv_sem=rs,
            device_id={"band": b, "lev": t}, device_id_type=MESH).start()
        return 0

    lax.fori_loop(1, NV, send_t, 0)

    pltpu.make_async_copy(recv2.at[0 : NXY - 1], recv2.at[0 : NXY - 1], r2).wait()
    c = jnp.zeros((64, 128), F32)
    for i in range(NX):
        part = recv2[NY * i : NY * i + NY].astype(F32).reshape(64, 128)
        c = jnp.where(group == i, pltpu.roll(part, lax.rem(i - x + NX, NX) * 32, 1), c)
    lane = lax.broadcasted_iota(jnp.int32, (64, 128), 1)
    row = lax.broadcasted_iota(jnp.int32, (64, 128), 0)
    c = jnp.where((row == 0) & (lane < 6), 0.5 * c, c)
    lane = lane & 31
    field = (lane - 6 * ((lane * 43) >> 8)) >> 1
    level_weight = lw[0]

    def synthesis(fields):
        lhs = jnp.concatenate([jnp.where(field == f, c, 0.0) for f in fields], axis=0).astype(BF16)
        z = jnp.dot(jnp.concatenate([lhs, lhs], axis=1), rhs[...], preferred_element_type=F32)
        return [
            jnp.sum(
                z[64 * i : 64 * i + 64, 0:LON_W] * ebuf[0] - z[64 * i : 64 * i + 64, LON_W:] * ebuf[1],
                axis=0, keepdims=True)
            for i in range(len(fields))
        ]

    winds = synthesis((0, 1))
    for f in range(2):
        for j in range(4):
            wrow[4 * f + j : 4 * f + j + 1, :] = level_weight * winds[f][:, 128 * j : 128 * j + 128]
    wsend[...] = wrow[...].astype(BF16)
    for t, _ in plane_partners(x, y):
        pltpu.make_async_remote_copy(
            src_ref=wsend, dst_ref=wrecv.at[xy], send_sem=sw, recv_sem=rw,
            device_id={"band": t * NZC + zc, "lev": v}, device_id_type=MESH).start()
    wrecv[xy] = wsend[...]
    for f, g in enumerate((*winds, *synthesis((2,)))):
        grid_o[0, f] = g

    pltpu.make_async_copy(wrecv.at[0 : NXY - 1], wrecv.at[0 : NXY - 1], rw).wait()
    wtab[...] = wrecv[...].astype(F32).reshape(8 * NXY, 128)
    table = jnp.concatenate(
        [
            jnp.concatenate([wtab[pl.ds(4 * f + j, NXY, stride=8), :] for j in range(4)], axis=1)
            for f in range(2)
        ],
        axis=0,
    ).astype(BF16)
    lat = lax.broadcasted_iota(jnp.int32, (NXY, 128), 0) * NZC + zc
    pl.semaphore_wait(told, NZC - 1)
    others = [lax.rem(v + d, NV) for d in (2, 1, 3, 0)]
    upper = zc // 4
    inner = lax.rem(zc // 2, 2)
    chip = inner + upper - 2 * inner * upper
    chips = [chip, 1 - chip, 2, 3]
    own = lax.rem(zc, 2)
    bands = [
        2 * (3 * upper + (1 - 2 * upper) * t) + (own if i == 0 else 1 - own) for t in chips for i in range(2)
    ]

    def products(g):
        return [jnp.dot(table, onehot[g * 2 + h], preferred_element_type=F32) for h in range(2)]

    ready = products(bands[0])
    for i, g in enumerate(bands):
        found = ready
        if i + 1 < NZC:
            ready = products(bands[i + 1])
        for line in range(4):
            h, j = line // 2, line % 2
            mine = lat == (coup_v[g, pl.ds(line, 1), :] >> 9)
            for f in range(2):
                picked = jnp.where(mine, found[h][32 * f : 32 * f + 32, 128 * j : 128 * j + 128], 0.0)
                rrow[i, 4 * f + line : 4 * f + line + 1, :] = jnp.sum(picked, axis=0, keepdims=True)
        rsend[g] = rrow[i].astype(BF16)
        for vv in others[: 4 if i else 3]:
            pltpu.make_async_remote_copy(
                src_ref=rsend.at[g], dst_ref=rrecv.at[zp], send_sem=sr, recv_sem=rr,
                device_id={"band": xy * NZC + g, "lev": vv}, device_id_type=MESH).start()
    rrecv[zp] = rsend[zc]

    pltpu.make_async_copy(trecv.at[0 : NV - 1], trecv.at[0 : NV - 1], rs).wait()
    total = tsum[...]
    for j in range(1, NV):
        total = total + trecv[lax.rem(v + j, NV)].astype(F32).reshape(HALF, 8, 128)
    tsum[...] = total

    pltpu.make_async_copy(rrecv.at[0 : NZ - 1], rrecv.at[0 : NZ - 1], rr).wait()
    wind = jnp.sum(rrecv[...].astype(F32), axis=0)
    turned = pltpu.roll(wind, 4, 0)
    low8 = lax.broadcasted_iota(jnp.int32, (8, 128), 0) < 4
    east8 = jnp.where(low8, -wind, turned)
    north8 = jnp.where(low8, -turned, wind)
    push = jnp.maximum(trig[0] * east8[None] + trig[1] * north8[None], 0.0)
    stress = jnp.sum(push * tsum[...], axis=0)
    mean = (stress + pltpu.roll(stress, 4, 0)) * land8[0] * (1.0 / (NF * ND))
    charnock = 0.011 + 0.5 * mean / (mean + 0.05 * (1.0 + wind * wind + turned * turned))
    char_o[...] = charnock[0:4]

    def result(f, _):
        s = state[f]
        s = s + s * (rate[f] * push)
        out_o[f, 0:HALF] = s[:, 4:8, :]
        out_o[f, HALF:] = s[:, 0:4, :]
        return 0

    lax.fori_loop(0, NF // NV, result, 0)

    halo_up.wait_send()
    halo_down.wait_send()
    pltpu.make_async_copy(coup_v.at[0:7], coup_v.at[0:7], sc).wait()
    pltpu.make_async_copy(recv1.at[0 : NZC - 1], recv1.at[0 : NZC - 1], s1).wait()
    pltpu.make_async_copy(recv2.at[0 : NXY - 1], recv2.at[0 : NXY - 1], s2).wait()
    pltpu.make_async_copy(wrecv.at[0 : NXY - 1], wrecv.at[0 : NXY - 1], sw).wait()
    pltpu.make_async_copy(rrecv.at[0 : NZ - 1], rrecv.at[0 : NZ - 1], sr).wait()
    pltpu.make_async_copy(trecv.at[0 : NV - 1], trecv.at[0 : NV - 1], ss).wait()


def write(grid, out, char, grid_o, out_o, char_o, sems):
    pieces = [(out.at[i : i + 3], out_o.at[i : i + 3]) for i in range(0, NF // NV, 3)]
    copies = [
        pltpu.make_async_copy(s, d, sems.at[i])
        for i, (s, d) in enumerate((*pieces, (grid, grid_o), (char, char_o)))
    ]
    for c in copies:
        c.start()
    for c in copies:
        c.wait()


def on_device(spectral, legendre, level_weights, coupling, land_sea, spectra, courant, growth_rate, breaking):
    spec = jnp.transpose(spectral, (0, 2, 3, 1, 4)).reshape(15, 2, N)
    hbm, vm = (pl.BlockSpec(memory_space=s) for s in (pltpu.HBM, pltpu.VMEM))
    sm = pltpu.SMEM
    dma = pltpu.SemaphoreType.DMA
    nf = NF // NV
    shapes = (
        jax.ShapeDtypeStruct((1, 3, 1, LON_W), F32),
        jax.ShapeDtypeStruct((nf, ND, 4, 128), F32),
        jax.ShapeDtypeStruct((4, 128), F32),
    )
    grid, out, char = pl.pallas_call(
        kernel,
        out_shape=shapes,
        in_specs=[pl.BlockSpec(memory_space=sm)] + [hbm] * 8,
        out_specs=(vm, vm, vm),
        scratch_shapes=[
            pltpu.VMEM((5, NLAT, N), BF16),
            pltpu.VMEM((15, 2, N), BF16),
            pltpu.VMEM((NZC, 4, 128), jnp.int32),
            pltpu.VMEM((4, 128), jnp.int32),
            pltpu.VMEM((nf, ND, 4, 128), BF16),
            pltpu.VMEM((32, N), F32),
            pltpu.VMEM((NZC, 8, 128), BF16),
            pltpu.VMEM((NZC, 8, 128), BF16),
            pltpu.VMEM((64, 128), F32),
            pltpu.VMEM((NY, 8, 128), BF16),
            pltpu.VMEM((NXY, 8, 128), BF16),
            pltpu.VMEM((256, 2 * LON_W), BF16),
            pltpu.VMEM((2, 64, LON_W), F32),
            pltpu.VMEM((8, 128), F32),
            pltpu.VMEM((8, 128), BF16),
            pltpu.VMEM((NXY, 8, 128), BF16),
            pltpu.VMEM((8 * NXY, 128), F32),
            pltpu.VMEM((2 * NZC, LON_W, 256), BF16),
            pltpu.VMEM((NZC, 8, 128), F32),
            pltpu.VMEM((NZC, 8, 128), BF16),
            pltpu.VMEM((NZ, 8, 128), BF16),
            pltpu.VMEM((2, nf, HALF, 4, 128), BF16),
            pltpu.VMEM((2, HALF, 8, 128), F32),
            pltpu.VMEM((2, HALF, 8, 128), F32),
            pltpu.VMEM((nf, HALF, 8, 128), F32),
            pltpu.VMEM((HALF, 8, 128), F32),
            pltpu.VMEM((HALF * 8, 128), BF16),
            pltpu.VMEM((NV, HALF * 8, 128), BF16),
            sm((nf,), F32), sm((nf,), F32), sm((nf,), F32),
            dma((5,)), dma((8,)),
            dma, dma, dma, dma, dma, dma, dma, dma,
            dma((2,)), dma((2,)), dma, dma, dma, dma,
            *[pltpu.SemaphoreType.REGULAR] * 5,
        ],
        compiler_params=pltpu.CompilerParams(
            collective_id=0, has_side_effects=True, vmem_limit_bytes=40 * 1024 * 1024
        ),
    )(
        level_weights,
        *(
            pltpu.with_memory_space_constraint(a, pltpu.HBM)
            for a in (spec, legendre, coupling, land_sea, spectra, courant, growth_rate, breaking)
        ),
    )
    grid, out, char = pl.pallas_call(
        write,
        out_shape=shapes,
        in_specs=[vm] * 3,
        out_specs=[hbm] * 3,
        scratch_shapes=[dma((5,))],
        compiler_params=pltpu.CompilerParams(vmem_limit_bytes=16 * 1024 * 1024),
    )(grid, out, char)
    return jnp.transpose(grid, (0, 2, 1, 3)), out, char


def solution(mesh):
    in_specs = (
        P("band", None, "lev", None, None),
        P("band", None, None),
        P("lev"),
        P("band", None),
        P("band", None),
        P("lev", None, "band", None),
        P("lev"),
        P("lev"),
        P("lev"),
    )
    out_specs = (P("band", "lev", None, None), P("lev", None, "band", None), P("band", None))
    return jax.shard_map(on_device, mesh=mesh, in_specs=in_specs, out_specs=out_specs, check_vma=False)
```
